512 devices in a mesh: src: 32 (over z, core), tgt: 16 (over x, y).
Axes of the slice: x: 4, y: 4, z: 16, core: 2. Of those that a mesh axis runs over, the one named last changes fastest.
Arguments:
- source_latents: bfloat16 [16384, 1024], P('src'), may hold values from -32 to 32
- target_latents: bfloat16 [16384, 1024], P('tgt'), may hold values from -32 to 32
Outputs:
- transported_targets: bfloat16 [16384, 1024], P('src', 'tgt')
- source_potential: float32 [16384], P('src')
- target_potential: float32 [16384], P('tgt')
The draws below stay inside these ranges and needn't reach their ends.
All inputs are finite; a program needn't handle non-finite values.
Results may differ from the reference program's by a relative error of at most 0.018.
Values may be sent and summed in bfloat16 or wider, within the bound.
A program may use at most 64 MiB of HBM per device.

```python
import math
import jax
import jax.numpy as jnp
from jax import lax

EMBED_DIMENSION = 1024
ITERS = 3
NS = 16384
NT = 16384


def latent_pair(seed_key, top_scale):
    keys = jax.random.split(seed_key, 7)
    normal_x = jax.random.normal(keys[0], (NS, EMBED_DIMENSION), jnp.float32)
    normal_y = jax.random.normal(keys[1], (NT, EMBED_DIMENSION), jnp.float32)
    row_scale = jnp.exp(jax.random.uniform(keys[5], (NS, 1), jnp.float32, 0.0, math.log(top_scale)))
    col_scale = jnp.exp(jax.random.uniform(keys[6], (NT, 1), jnp.float32, 0.0, math.log(top_scale)))
    sources = normal_x * row_scale
    targets = normal_y * col_scale
    picked_rows = jnp.arange(8) * (NS // 8)
    picked_cols = jnp.arange(8) * (NT // 8)
    targets = targets.at[picked_cols + 1].set(targets[picked_cols + 1])
    sources = sources.at[picked_rows].set(sources[picked_rows])
    sources = sources.at[picked_rows + 1].multiply(5.0)
    return (jnp.clip(sources, -32.0, 32.0), jnp.clip(targets, -32.0, 32.0))


def draw_source_latents(key, part):
    latents = latent_pair(key, 2.0)
    return latents[0].astype(jnp.bfloat16)


def draw_target_latents(key, part):
    latents = latent_pair(key, 2.0)
    return latents[1].astype(jnp.bfloat16)


def setup_inputs(seed: int = 0) -> dict:
    arg_keys = jax.random.split(jax.random.key(seed), 3)
    source_latents = draw_source_latents(jax.random.fold_in(arg_keys[2], 71), 0)
    target_latents = draw_target_latents(jax.random.fold_in(arg_keys[2], 71), 0)
    return {"source_latents": source_latents, "target_latents": target_latents}


def reference(source_latents, target_latents):
    regularizer_strength = 1.28 / math.sqrt(EMBED_DIMENSION)
    row_count = math.gcd(NS, 512)
    sources = source_latents.astype(jnp.float32)
    targets = target_latents.astype(jnp.float32)
    source_sq = lax.optimization_barrier(jnp.sum(sources * sources, axis=1)) / EMBED_DIMENSION
    target_sq = lax.optimization_barrier(jnp.sum(targets * targets, axis=1)) / EMBED_DIMENSION
    source_blocks = sources.reshape(NS // row_count, row_count, EMBED_DIMENSION)
    sq_blocks = source_sq.reshape(NS // row_count, row_count)
    source_logarithmic_mass = math.log(NS)
    target_logarithmic_mass = math.log(NT)

    def cost_of(row_block, rows_sq):
        cross_term = jnp.dot(row_block, targets.T, precision=lax.Precision.HIGHEST)
        return rows_sq[:, None] + target_sq[None, :] - 2.0 / EMBED_DIMENSION * cross_term

    def source_softmax_normalizer(kernel_exponent_array):
        top_score = lax.optimization_barrier(jnp.max(kernel_exponent_array, axis=1))
        return top_score + jnp.log(lax.optimization_barrier(jnp.sum(jnp.exp(kernel_exponent_array - top_score[:, None]), axis=1)))

    def sweep_once(target_dual_variable):

        def advance(running, block_pair):
            target_peak_value, target_aggregate_mass = running
            row_block, rows_sq = block_pair
            pairwise_price_piece = cost_of(row_block, rows_sq)
            source_dual_variable = -regularizer_strength * target_logarithmic_mass - regularizer_strength * source_softmax_normalizer((target_dual_variable[None, :] - pairwise_price_piece) / regularizer_strength)
            kernel_exponent_array = (source_dual_variable[:, None] - pairwise_price_piece) / regularizer_strength
            new_peak = jnp.maximum(target_peak_value, lax.optimization_barrier(jnp.max(kernel_exponent_array, axis=0)))
            target_aggregate_mass = target_aggregate_mass * jnp.exp(target_peak_value - new_peak) + lax.optimization_barrier(jnp.sum(jnp.exp(kernel_exponent_array - new_peak[None, :]), axis=0))
            return ((new_peak, target_aggregate_mass), source_dual_variable)
        initial = (jnp.full((NT,), -jnp.inf, jnp.float32), jnp.zeros((NT,), jnp.float32))
        (target_peak_value, target_aggregate_mass), source_dual_variable = lax.scan(advance, initial, (source_blocks, sq_blocks))
        target_dual_variable = -regularizer_strength * source_logarithmic_mass - regularizer_strength * (target_peak_value + jnp.log(target_aggregate_mass))
        return (source_dual_variable.reshape(NS), target_dual_variable)
    target_dual_variable = jnp.zeros((NT,), jnp.float32)
    source_dual_variable = jnp.zeros((NS,), jnp.float32)
    for sweep_index in range(ITERS):
        source_dual_variable, target_dual_variable = sweep_once(target_dual_variable)

    def transport(block_pair):
        row_block, rows_sq = block_pair
        pairwise_price_piece = cost_of(row_block, rows_sq)
        kernel_exponent_array = (target_dual_variable[None, :] - pairwise_price_piece) / regularizer_strength
        row_level = source_softmax_normalizer(kernel_exponent_array)
        weights = jnp.exp(kernel_exponent_array - row_level[:, None]).astype(jnp.bfloat16)
        weights = lax.optimization_barrier(weights).astype(jnp.float32)
        return jnp.dot(weights, targets, precision=lax.Precision.HIGHEST)
    transported = lax.map(transport, (source_blocks, sq_blocks)).reshape(NS, EMBED_DIMENSION).astype(jnp.bfloat16)
    return (transported, source_dual_variable, target_dual_variable)
```

```python
import functools
import math

import jax
import jax.numpy as jnp
from jax import lax
from jax.experimental import pallas as pl
from jax.experimental.pallas import tpu as pltpu
from jax.sharding import PartitionSpec as P

ITERS = 3
LOG2E = math.log2(math.e)
LANES = 128
F32 = jnp.float32
BF16 = jnp.bfloat16
NT_DIMS = (((1,), (1,)), ((), ()))


def ring_distance(k, n):
    return min(k, n - k)


def log2(x):
    return jnp.log(x) * LOG2E


def combine(parts):
    top = functools.reduce(jnp.maximum, parts)
    total = functools.reduce(jnp.add, [jnp.exp2(p - top) for p in parts])
    return top + log2(total)


def square_sums(block_ref, start, out_ref, row):
    width = block_ref.shape[1]
    total = jnp.zeros((LANES, LANES), F32)
    for c in range(width // LANES):
        piece = block_ref[pl.ds(start, LANES), c * LANES : (c + 1) * LANES].astype(F32)
        total = total + piece * piece
    out_ref[row : row + 1, :] = jnp.sum(total.T, axis=0, keepdims=True)


def kernel(
    cfg,
    src_hbm,
    tgt_hbm,
    moved_ref,
    f_ref,
    g_ref,
    a,
    b,
    b_t,
    scores,
    part,
    column,
    weights,
    sums,
    arrived,
    h_ref,
    u_ref,
    ss_ref,
    tt_ref,
    peak_ref,
    mass_ref,
    own_lse,
    t_send,
    t_recv,
    c_send,
    c_recv,
    z_send,
    z_recv,
    load_sem,
    t_ssem,
    t_rsem,
    c_ssem,
    c_rsem,
    z_ssem,
    z_rsem,
    m_ssem,
    m_rsem,
):
    n_z, n_x, n_y, eps, log2_rows, log2_cols = cfg
    rows, depth = a.shape
    cols = b.shape[0]
    row_groups, col_groups = rows // LANES, cols // LANES
    s_me, t_me = lax.axis_index("src"), lax.axis_index("tgt")
    z_me, core_me = s_me // 2, s_me % 2
    x_me, y_me = t_me // n_y, t_me % n_y
    feats = depth // (n_x * n_y)

    z_peers = []
    for k in sorted(range(1, n_z), key=lambda k: -ring_distance(k, n_z)):
        z_peers.append({"src": ((z_me + k) % n_z) * 2 + core_me, "tgt": t_me})
    sibling = {"src": z_me * 2 + (1 - core_me), "tgt": t_me}
    steps = [(dx, dy) for dx in range(n_x) for dy in range(n_y) if dx or dy]
    steps.sort(key=lambda d: (-ring_distance(d[0], n_x), -ring_distance(d[1], n_y)))
    t_index = [((x_me + dx) % n_x) * n_y + (y_me + dy) % n_y for dx, dy in steps]
    far = sorted(
        range(len(steps)),
        key=lambda k: -ring_distance(steps[k][0], n_x) - ring_distance(steps[k][1], n_y),
    )

    barrier = pltpu.get_barrier_semaphore()
    everyone = z_peers + [{"src": s_me, "tgt": t_index[k]} for k in far] + [sibling]
    for peer in everyone:
        pl.semaphore_signal(
            barrier, inc=1, device_id=peer, device_id_type=pl.DeviceIdType.MESH
        )

    quarter = cols // 4
    loads = [pltpu.make_async_copy(src_hbm, a, load_sem.at[4])]
    for q in range(4):
        piece = pl.ds(q * quarter, quarter)
        loads.append(pltpu.make_async_copy(tgt_hbm.at[piece], b.at[piece], load_sem.at[q]))
    for copy in loads:
        copy.start()
    loads[0].wait()
    for q in range(4):
        loads[1 + q].wait()
        dot = lax.dot_general(
            a[...],
            b[q * quarter : (q + 1) * quarter, :],
            NT_DIMS,
            preferred_element_type=F32,
        )
        scores[:, q * quarter : (q + 1) * quarter] = dot * (2.0 * LOG2E / (depth * eps))
        for k in range(quarter // LANES):
            block = q * (quarter // LANES) + k
            square_sums(b, block * LANES, tt_ref, block)
    h_ref[...] = tt_ref[...] * (-LOG2E / (depth * eps))

    def rows_pass(out_ref):
        shift = [
            jnp.broadcast_to(h_ref[c : c + 1, :], (8, LANES)) for c in range(col_groups)
        ]

        def some_rows(block, carry):
            for k in range(4):
                at = pl.ds(pl.multiple_of(block * 32 + k * 8, 8), 8)
                v = [
                    scores[at, c * LANES : (c + 1) * LANES] + shift[c]
                    for c in range(col_groups)
                ]
                part[at, :] = combine(v)
            return carry

        lax.fori_loop(0, rows // 32, some_rows, 0)
        for r in range(row_groups):
            x = part[r * LANES : (r + 1) * LANES, :].T
            top = jnp.max(x, axis=0, keepdims=True)
            out_ref[r : r + 1, :] = top + log2(
                jnp.sum(jnp.exp2(x - top), axis=0, keepdims=True)
            )

    def to_column(ref):
        for r in range(row_groups):
            column[r * LANES : (r + 1) * LANES, :] = jnp.broadcast_to(
                ref[r : r + 1, :], (LANES, LANES)
            ).T

    def start_rows_exchange(i):
        for k in far:
            pltpu.make_async_remote_copy(
                src_ref=t_send.at[i],
                dst_ref=t_recv.at[i, k],
                send_sem=t_ssem.at[i],
                recv_sem=t_rsem.at[i],
                device_id={"src": s_me, "tgt": t_index[k]},
                device_id_type=pl.DeviceIdType.MESH,
            ).start()

    def wait_bytes(ref, sem):
        pltpu.make_async_copy(ref, ref, sem).wait()

    def columns_pass(out_ref):
        shape = (8, LANES)
        low = jnp.full(shape, -3.0e38, F32)
        start = tuple([low] * col_groups + [jnp.zeros(shape, F32)] * col_groups)

        def some_rows(block, carry):
            tops, totals = list(carry[:col_groups]), list(carry[col_groups:])
            at = [pl.ds(pl.multiple_of(block * 64 + k * 8, 8), 8) for k in range(8)]
            u = [column[p, :] for p in at]
            for c in range(col_groups):
                v = [scores[p, c * LANES : (c + 1) * LANES] + w for p, w in zip(at, u)]
                top = functools.reduce(jnp.maximum, v + [tops[c]])
                mass = functools.reduce(jnp.add, [jnp.exp2(p - top) for p in v])
                totals[c] = totals[c] * jnp.exp2(tops[c] - top) + mass
                tops[c] = top
            return tuple(tops + totals)

        done = lax.fori_loop(0, rows // 64, some_rows, start)
        for c in range(col_groups):
            peak_ref[c * 8 : (c + 1) * 8, :] = done[c]
            mass_ref[c * 8 : (c + 1) * 8, :] = done[col_groups + c]
        peaks = [peak_ref[pl.ds(r, col_groups, stride=8), :] for r in range(8)]
        masses = [mass_ref[pl.ds(r, col_groups, stride=8), :] for r in range(8)]
        top = functools.reduce(jnp.maximum, peaks)
        total = functools.reduce(
            jnp.add, [m * jnp.exp2(p - top) for p, m in zip(peaks, masses)]
        )
        out_ref[...] = top + log2(total)

    def sweep(i, carry):
        rows_pass(t_send.at[i])

        @pl.when(i == 0)
        def _():
            pl.semaphore_wait(barrier, len(everyone))

        start_rows_exchange(i)

        @pl.when(i == 0)
        def _():
            for r in range(row_groups):
                square_sums(a, r * LANES, ss_ref, r)

            def turn(block, carry):
                at = pl.ds(pl.multiple_of(block * LANES, LANES), LANES)
                for c in range(depth // LANES):
                    b_t[c * LANES : (c + 1) * LANES, at] = b[
                        at, c * LANES : (c + 1) * LANES
                    ].T
                return carry

            lax.fori_loop(0, col_groups, turn, 0)

        wait_bytes(t_recv.at[i], t_rsem.at[i])
        u_ref[...] = -log2_cols - combine(
            [t_send[i]] + [t_recv[i, k] for k in range(len(steps))]
        )
        to_column(u_ref)
        columns_pass(c_send.at[i])
        copy = pltpu.make_async_remote_copy(
            src_ref=c_send.at[i],
            dst_ref=c_recv.at[i],
            send_sem=c_ssem.at[i],
            recv_sem=c_rsem.at[i],
            device_id=sibling,
            device_id_type=pl.DeviceIdType.MESH,
        )
        copy.start()
        copy.wait_recv()
        z_send[i] = combine([c_send[i], c_recv[i]])
        for k, peer in enumerate(z_peers):
            pltpu.make_async_remote_copy(
                src_ref=z_send.at[i],
                dst_ref=z_recv.at[i, k],
                send_sem=z_ssem.at[i],
                recv_sem=z_rsem.at[i],
                device_id=peer,
                device_id_type=pl.DeviceIdType.MESH,
            ).start()
        wait_bytes(z_recv.at[i], z_rsem.at[i])
        h_ref[...] = -log2_rows - combine(
            [z_send[i]] + [z_recv[i, k] for k in range(len(z_peers))]
        )
        return carry

    lax.fori_loop(0, ITERS, sweep, 0)

    rows_pass(t_send.at[ITERS])
    start_rows_exchange(ITERS)
    to_column(t_send.at[ITERS])
    shift = [
        jnp.broadcast_to(h_ref[c : c + 1, :], (16, LANES)) for c in range(col_groups)
    ]

    def some_weights(block, carry):
        for k in range(2):
            at = pl.ds(pl.multiple_of(block * 32 + k * 16, 16), 16)
            level = column[at, :]
            for c in range(col_groups):
                v = scores[at, c * LANES : (c + 1) * LANES] + shift[c]
                weights[at, c * LANES : (c + 1) * LANES] = jnp.exp2(v - level).astype(BF16)
        return carry

    lax.fori_loop(0, rows // 32, some_weights, 0)

    per_x = n_y * feats
    for dx in sorted(range(n_x), key=lambda d: -ring_distance(d, n_x)):
        start = pl.multiple_of(((x_me + dx) % n_x) * per_x, per_x)
        dot = lax.dot_general(
            b_t[pl.ds(start, per_x), :],
            weights[...],
            NT_DIMS,
            preferred_element_type=F32,
        )
        sums[pl.ds(start, per_x), :] = dot.astype(BF16)
        for k, step in enumerate(steps):
            if step[0] == dx:
                pltpu.make_async_remote_copy(
                    src_ref=sums.at[
                        pl.ds(pl.multiple_of(t_index[k] * feats, feats), feats)
                    ],
                    dst_ref=arrived.at[k],
                    send_sem=m_ssem.at[k],
                    recv_sem=m_rsem.at[k],
                    device_id={"src": s_me, "tgt": t_index[k]},
                    device_id_type=pl.DeviceIdType.MESH,
                ).start()

    f_ref[...] = ss_ref[...] * (1.0 / depth) + u_ref[...] * (eps / LOG2E)
    g_ref[...] = tt_ref[...] * (1.0 / depth) + h_ref[...] * (eps / LOG2E)

    wait_bytes(t_recv.at[ITERS], t_rsem.at[ITERS])
    level = combine([t_send[ITERS]] + [t_recv[ITERS, k] for k in range(len(steps))])
    own_lse[...] = jnp.exp2(t_send[ITERS] - level)
    for k in range(len(steps)):
        t_recv[ITERS, k] = jnp.exp2(t_recv[ITERS, k] - level)
    mine = pl.ds(pl.multiple_of(t_me * feats, feats), feats)
    for r in range(row_groups):
        lane = slice(r * LANES, (r + 1) * LANES)
        moved_ref[:, lane] = sums[mine, lane].astype(F32) * own_lse[r : r + 1, :]
    for k in sorted(
        range(len(steps)),
        key=lambda k: ring_distance(steps[k][0], n_x) + ring_distance(steps[k][1], n_y),
    ):
        wait_bytes(arrived.at[k], m_rsem.at[k])
        for r in range(row_groups):
            lane = slice(r * LANES, (r + 1) * LANES)
            moved_ref[:, lane] += (
                arrived[k, :, lane].astype(F32) * t_recv[ITERS, k, r : r + 1, :]
            )

    for i in range(ITERS):
        wait_bytes(c_send.at[i], c_ssem.at[i])
        wait_bytes(z_recv.at[i], z_ssem.at[i])
    for i in range(ITERS + 1):
        wait_bytes(t_recv.at[i], t_ssem.at[i])
    for k in range(len(steps)):
        wait_bytes(arrived.at[k], m_ssem.at[k])


def local(cfg, source_latents, target_latents):
    n_z, n_x, n_y = cfg[:3]
    rows, depth = source_latents.shape
    cols = target_latents.shape[0]
    feats = depth // (n_x * n_y)
    row_groups, col_groups = rows // LANES, cols // LANES
    t_peers, z_peers = n_x * n_y - 1, n_z - 1
    vmem = pl.BlockSpec(memory_space=pltpu.VMEM)
    hbm = pl.BlockSpec(memory_space=pl.ANY)
    dma = pltpu.SemaphoreType.DMA
    moved, f, g = pl.pallas_call(
        functools.partial(kernel, cfg),
        out_shape=(
            jax.ShapeDtypeStruct((feats, rows), F32),
            jax.ShapeDtypeStruct((row_groups, LANES), F32),
            jax.ShapeDtypeStruct((col_groups, LANES), F32),
        ),
        in_specs=[hbm, hbm],
        out_specs=(vmem, vmem, vmem),
        scratch_shapes=[
            pltpu.VMEM((rows, depth), BF16),
            pltpu.VMEM((cols, depth), BF16),
            pltpu.VMEM((depth, cols), BF16),
            pltpu.VMEM((rows, cols), F32),
            pltpu.VMEM((rows, LANES), F32),
            pltpu.VMEM((rows, LANES), F32),
            pltpu.VMEM((rows, cols), BF16),
            pltpu.VMEM((depth, rows), BF16),
            pltpu.VMEM((t_peers, feats, rows), BF16),
            pltpu.VMEM((col_groups, LANES), F32),
            pltpu.VMEM((row_groups, LANES), F32),
            pltpu.VMEM((row_groups, LANES), F32),
            pltpu.VMEM((col_groups, LANES), F32),
            pltpu.VMEM((col_groups * 8, LANES), F32),
            pltpu.VMEM((col_groups * 8, LANES), F32),
            pltpu.VMEM((row_groups, LANES), F32),
            pltpu.VMEM((ITERS + 1, row_groups, LANES), F32),
            pltpu.VMEM((ITERS + 1, t_peers, row_groups, LANES), F32),
            pltpu.VMEM((ITERS, col_groups, LANES), F32),
            pltpu.VMEM((ITERS, col_groups, LANES), F32),
            pltpu.VMEM((ITERS, col_groups, LANES), F32),
            pltpu.VMEM((ITERS, z_peers, col_groups, LANES), F32),
            dma((5,)),
            dma((ITERS + 1,)),
            dma((ITERS + 1,)),
            dma((ITERS,)),
            dma((ITERS,)),
            dma((ITERS,)),
            dma((ITERS,)),
            dma((t_peers,)),
            dma((t_peers,)),
        ],
        compiler_params=pltpu.CompilerParams(
            collective_id=0, has_side_effects=True, vmem_limit_bytes=40 << 20
        ),
        name="transport",
    )(source_latents, target_latents)
    return moved.T.astype(BF16), f.reshape(rows), g.reshape(cols)


def solution(mesh):
    n_src, n_tgt = mesh.shape["src"], mesh.shape["tgt"]
    n_x = math.isqrt(n_tgt)

    def whole(source_latents, target_latents):
        eps = 1.28 / math.sqrt(source_latents.shape[1])
        cfg = (
            n_src // 2,
            n_x,
            n_tgt // n_x,
            eps,
            math.log2(source_latents.shape[0]),
            math.log2(target_latents.shape[0]),
        )
        return jax.shard_map(
            functools.partial(local, cfg),
            mesh=mesh,
            in_specs=(P("src", None), P("tgt", None)),
            out_specs=(P("src", "tgt"), P("src"), P("tgt")),
            check_vma=False,
        )(source_latents, target_latents)

    return whole
```

```python
import functools
import math

import jax
import jax.numpy as jnp
from jax import lax
from jax.experimental import pallas as pl
from jax.experimental.pallas import tpu as pltpu
from jax.sharding import PartitionSpec as P

ITERS = 3
QUARTERS = 4
CHUNKS = 2
LOG2E = math.log2(math.e)
LANES = 128
F32 = jnp.float32
BF16 = jnp.bfloat16
NT_DIMS = (((1,), (1,)), ((), ()))


def ring_distance(k, n):
    return min(k, n - k)


def log2(x):
    return jnp.log(x) * LOG2E


def combine(parts):
    top = functools.reduce(jnp.maximum, parts)
    total = functools.reduce(jnp.add, [jnp.exp2(p - top) for p in parts])
    return top + log2(total)


def square_sums(block_ref, start, out_ref, row):
    width = block_ref.shape[1]
    total = jnp.zeros((LANES, LANES), F32)
    for c in range(width // LANES):
        piece = block_ref[pl.ds(start, LANES), c * LANES : (c + 1) * LANES].astype(F32)
        total = total + piece * piece
    out_ref[row : row + 1, :] = jnp.sum(total.T, axis=0, keepdims=True)


def kernel(
    cfg,
    src_hbm,
    tgt_hbm,
    moved_ref,
    f_ref,
    g_ref,
    a,
    b,
    b_t,
    scores,
    part,
    mass,
    column,
    weights,
    sums,
    first_in,
    second_out,
    second_in,
    h_ref,
    u_ref,
    ss_ref,
    tt_ref,
    peak_ref,
    mass_ref,
    own_scale,
    t_send,
    t_recv,
    c_send,
    c_recv,
    z_send,
    z_recv,
    load_sem,
    t_ssem,
    t_rsem,
    c_ssem,
    c_rsem,
    z_ssem,
    z_rsem,
    m_ssem,
    m_rsem,
    n_ssem,
    n_rsem,
):
    n_z, n_x, n_y, eps, log2_rows, log2_cols = cfg
    rows, depth = a.shape
    cols = b.shape[0]
    row_groups, col_groups = rows // LANES, cols // LANES
    s_me, t_me = lax.axis_index("src"), lax.axis_index("tgt")
    z_me, core_me = s_me // 2, s_me % 2
    x_me, y_me = t_me // n_y, t_me % n_y
    half = depth // (n_x * n_y) // 2
    chunk = rows // CHUNKS

    z_peers = []
    for k in sorted(range(1, n_z), key=lambda k: -ring_distance(k, n_z)):
        z_peers.append({"src": ((z_me + k) % n_z) * 2 + core_me, "tgt": t_me})
    sibling = {"src": z_me * 2 + (1 - core_me), "tgt": t_me}
    steps = [(dx, dy) for dx in range(n_x) for dy in range(n_y) if dx or dy]
    steps.sort(key=lambda d: (-ring_distance(d[0], n_x), -ring_distance(d[1], n_y)))
    t_index = [((x_me + dx) % n_x) * n_y + (y_me + dy) % n_y for dx, dy in steps]
    far = sorted(
        range(len(steps)),
        key=lambda k: -ring_distance(steps[k][0], n_x) - ring_distance(steps[k][1], n_y),
    )

    barrier = pltpu.get_barrier_semaphore()
    everyone = z_peers + [{"src": s_me, "tgt": t_index[k]} for k in far] + [sibling]
    for peer in everyone:
        pl.semaphore_signal(
            barrier, inc=1, device_id=peer, device_id_type=pl.DeviceIdType.MESH
        )

    quarter = cols // QUARTERS
    loads = [pltpu.make_async_copy(src_hbm, a, load_sem.at[QUARTERS])]
    for q in range(QUARTERS):
        piece = pl.ds(q * quarter, quarter)
        loads.append(pltpu.make_async_copy(tgt_hbm.at[piece], b.at[piece], load_sem.at[q]))
    for copy in loads:
        copy.start()
    for q in range(QUARTERS):
        loads[1 + q].wait()
        blocks = range(q * quarter // LANES, (q + 1) * quarter // LANES)
        for c in blocks:
            square_sums(b, c * LANES, tt_ref, c)
        if q == 0:
            loads[0].wait()
        dot = lax.dot_general(
            a[...],
            b[q * quarter : (q + 1) * quarter, :],
            NT_DIMS,
            preferred_element_type=F32,
        )
        scores[:, q * quarter : (q + 1) * quarter] = dot * (2.0 * LOG2E / (depth * eps))
    h_ref[...] = tt_ref[...] * (-LOG2E / (depth * eps))

    def rows_pass(out_ref):
        shift = [
            jnp.broadcast_to(h_ref[c : c + 1, :], (8, LANES)) for c in range(col_groups)
        ]

        def some_rows(block, carry):
            for k in range(4):
                at = pl.ds(pl.multiple_of(block * 32 + k * 8, 8), 8)
                v = [
                    scores[at, c * LANES : (c + 1) * LANES] + shift[c]
                    for c in range(col_groups)
                ]
                part[at, :] = combine(v)
            return carry

        lax.fori_loop(0, rows // 32, some_rows, 0)
        for r in range(row_groups):
            x = part[r * LANES : (r + 1) * LANES, :].T
            top = jnp.max(x, axis=0, keepdims=True)
            out_ref[r : r + 1, :] = top + log2(
                jnp.sum(jnp.exp2(x - top), axis=0, keepdims=True)
            )

    def to_column(ref):
        for r in range(row_groups):
            column[r * LANES : (r + 1) * LANES, :] = jnp.broadcast_to(
                ref[r : r + 1, :], (LANES, LANES)
            ).T

    def start_rows_exchange(i):
        for k in far:
            pltpu.make_async_remote_copy(
                src_ref=t_send.at[i],
                dst_ref=t_recv.at[i, k],
                send_sem=t_ssem.at[i],
                recv_sem=t_rsem.at[i],
                device_id={"src": s_me, "tgt": t_index[k]},
                device_id_type=pl.DeviceIdType.MESH,
            ).start()

    def wait_bytes(ref, sem):
        pltpu.make_async_copy(ref, ref, sem).wait()

    def columns_pass(out_ref):
        shape = (8, LANES)
        low = jnp.full(shape, -3.0e38, F32)
        start = tuple([low] * col_groups + [jnp.zeros(shape, F32)] * col_groups)

        def some_rows(block, carry):
            tops, totals = list(carry[:col_groups]), list(carry[col_groups:])
            at = [pl.ds(pl.multiple_of(block * 64 + k * 8, 8), 8) for k in range(8)]
            u = [column[p, :] for p in at]
            for c in range(col_groups):
                v = [scores[p, c * LANES : (c + 1) * LANES] + w for p, w in zip(at, u)]
                top = functools.reduce(jnp.maximum, v + [tops[c]])
                mass = functools.reduce(jnp.add, [jnp.exp2(p - top) for p in v])
                totals[c] = totals[c] * jnp.exp2(tops[c] - top) + mass
                tops[c] = top
            return tuple(tops + totals)

        done = lax.fori_loop(0, rows // 64, some_rows, start)
        for c in range(col_groups):
            peak_ref[c * 8 : (c + 1) * 8, :] = done[c]
            mass_ref[c * 8 : (c + 1) * 8, :] = done[col_groups + c]
        peaks = [peak_ref[pl.ds(r, col_groups, stride=8), :] for r in range(8)]
        masses = [mass_ref[pl.ds(r, col_groups, stride=8), :] for r in range(8)]
        top = functools.reduce(jnp.maximum, peaks)
        total = functools.reduce(
            jnp.add, [m * jnp.exp2(p - top) for p, m in zip(peaks, masses)]
        )
        out_ref[...] = top + log2(total)

    rows_pass(t_send.at[0])
    pl.semaphore_wait(barrier, len(everyone))
    start_rows_exchange(0)

    for r in range(row_groups):
        square_sums(a, r * LANES, ss_ref, r)
    order = sorted(range(n_x), key=lambda d: -ring_distance(d, n_x))

    def position(along):
        return sum(jnp.where(along == e, o, 0) for o, e in enumerate(order))

    def turn(block, carry):
        at = pl.ds(pl.multiple_of(block * LANES, LANES), LANES)
        for c in range(depth // LANES):
            turned = b[at, c * LANES : (c + 1) * LANES].T
            for o in range(LANES // half):
                owner, second = divmod(c * (LANES // half) + o, 2)
                ox, oy = owner // n_y, owner % n_y
                if second:
                    row = position((oy - y_me + n_y) % n_y) * (2 * n_y) + n_y + ox
                else:
                    row = position((ox - x_me + n_x) % n_x) * (2 * n_y) + oy
                b_t[pl.ds(pl.multiple_of(row * half, half), half), at] = turned[
                    o * half : (o + 1) * half
                ]
        return carry

    lax.fori_loop(0, col_groups, turn, 0)

    def sweep(i, carry):
        wait_bytes(t_recv.at[i], t_rsem.at[i])
        u_ref[...] = -log2_cols - combine(
            [t_send[i]] + [t_recv[i, k] for k in range(len(steps))]
        )
        to_column(u_ref)
        columns_pass(c_send.at[i])
        copy = pltpu.make_async_remote_copy(
            src_ref=c_send.at[i],
            dst_ref=c_recv.at[i],
            send_sem=c_ssem.at[i],
            recv_sem=c_rsem.at[i],
            device_id=sibling,
            device_id_type=pl.DeviceIdType.MESH,
        )
        copy.start()
        copy.wait_recv()
        z_send[i] = combine([c_send[i], c_recv[i]])
        for k, peer in enumerate(z_peers):
            pltpu.make_async_remote_copy(
                src_ref=z_send.at[i],
                dst_ref=z_recv.at[i, k],
                send_sem=z_ssem.at[i],
                recv_sem=z_rsem.at[i],
                device_id=peer,
                device_id_type=pl.DeviceIdType.MESH,
            ).start()
        wait_bytes(z_recv.at[i], z_rsem.at[i])
        h_ref[...] = -log2_rows - combine(
            [z_send[i]] + [z_recv[i, k] for k in range(len(z_peers))]
        )
        rows_pass(t_send.at[i + 1])
        start_rows_exchange(i + 1)
        return carry

    lax.fori_loop(0, ITERS, sweep, 0)

    to_column(t_send.at[ITERS])
    shift = [
        jnp.broadcast_to(h_ref[c : c + 1, :], (16, LANES)) for c in range(col_groups)
    ]

    def some_weights(block, carry):
        for k in range(2):
            at = pl.ds(pl.multiple_of(block * 32 + k * 16, 16), 16)
            level = column[at, :]
            for c in range(col_groups):
                v = scores[at, c * LANES : (c + 1) * LANES] + shift[c]
                weights[at, c * LANES : (c + 1) * LANES] = jnp.exp2(v - level).astype(BF16)
        return carry

    band = n_y * half

    def plane_peer(kind, step):
        if kind == 0:
            return {"src": s_me, "tgt": ((x_me + step) % n_x) * n_y + y_me}
        return {"src": s_me, "tgt": x_me * n_y + (y_me + step) % n_y}

    for n in range(CHUNKS):
        per = rows // 32 // CHUNKS
        lax.fori_loop(n * per, (n + 1) * per, some_weights, 0)
        for o in range(0, n_x, 2):
            at = pl.ds(o * 2 * band, 4 * band)
            dot = lax.dot_general(
                b_t[at, :],
                weights[n * chunk : (n + 1) * chunk, :],
                NT_DIMS,
                preferred_element_type=F32,
            )
            sums[n, at, :] = dot.astype(BF16)
            for p in (o, o + 1):
                for kind in range(2):
                    if order[p]:
                        pltpu.make_async_remote_copy(
                            src_ref=sums.at[n, pl.ds((2 * p + kind) * band, band)],
                            dst_ref=first_in.at[n, kind, order[p] - 1],
                            send_sem=m_ssem.at[n],
                            recv_sem=m_rsem.at[n],
                            device_id=plane_peer(kind, order[p]),
                            device_id_type=pl.DeviceIdType.MESH,
                        ).start()

    f_ref[...] = ss_ref[...] * (1.0 / depth) + u_ref[...] * (eps / LOG2E)
    g_ref[...] = tt_ref[...] * (1.0 / depth) + h_ref[...] * (eps / LOG2E)

    wait_bytes(t_recv.at[ITERS], t_rsem.at[ITERS])
    level = combine([t_send[ITERS]] + [t_recv[ITERS, k] for k in range(len(steps))])
    own_scale[...] = jnp.exp2(t_send[ITERS] - level)
    along = [[steps.index((d, 0)) for d in range(1, n_x)], [steps.index((0, d)) for d in range(1, n_y)]]
    for line in along:
        for k in line:
            t_recv[ITERS, k] = jnp.exp2(t_recv[ITERS, k] - level)

    own = order.index(0)
    lanes = [slice(r * LANES, (r + 1) * LANES) for r in range(chunk // LANES)]
    for n in range(CHUNKS):
        wait_bytes(first_in.at[n], m_rsem.at[n])
        for kind in range(2):
            for r, lane in enumerate(lanes):
                g = n * (chunk // LANES) + r
                at = pl.ds((2 * own + kind) * band, band)
                total = sums[n, at, lane].astype(F32) * own_scale[g : g + 1, :]
                for j, k in enumerate(along[kind]):
                    total += first_in[n, kind, j, :, lane].astype(F32) * t_recv[ITERS, k, g : g + 1, :]
                second_out[n, kind, :, lane] = total.astype(BF16)
            for step in order:
                if step:
                    to = (y_me + step) % n_y if kind == 0 else (x_me + step) % n_x
                    pltpu.make_async_remote_copy(
                        src_ref=second_out.at[n, kind, pl.ds(pl.multiple_of(to * half, half), half)],
                        dst_ref=second_in.at[n, kind, step - 1],
                        send_sem=n_ssem.at[n],
                        recv_sem=n_rsem.at[n],
                        device_id=plane_peer(1 - kind, step),
                        device_id_type=pl.DeviceIdType.MESH,
                    ).start()
    for n in range(CHUNKS):
        wait_bytes(second_in.at[n], n_rsem.at[n])
        for kind in range(2):
            me = y_me if kind == 0 else x_me
            mine = pl.ds(pl.multiple_of(me * half, half), half)
            for r, lane in enumerate(lanes):
                total = second_out[n, kind, mine, lane].astype(F32)
                for j in range(n_x - 1):
                    total += second_in[n, kind, j, :, lane].astype(F32)
                at = n * chunk + r * LANES
                moved_ref[kind * half : (kind + 1) * half, at : at + LANES] = total.astype(BF16)

    for i in range(ITERS):
        wait_bytes(c_send.at[i], c_ssem.at[i])
        wait_bytes(z_recv.at[i], z_ssem.at[i])
    for i in range(ITERS + 1):
        wait_bytes(t_recv.at[i], t_ssem.at[i])
    for n in range(CHUNKS):
        wait_bytes(first_in.at[n], m_ssem.at[n])
        wait_bytes(second_in.at[n], n_ssem.at[n])


def hand_out(moved_ref, f_ref, g_ref, *outs_and_sem):
    *outs, sem = outs_and_sem
    copies = [
        pltpu.make_async_copy(ref, out, sem.at[k])
        for k, (ref, out) in enumerate(zip((moved_ref, f_ref, g_ref), outs))
    ]
    for copy in copies:
        copy.start()
    for copy in copies:
        copy.wait()


def local(cfg, source_latents, target_latents):
    n_z, n_x, n_y = cfg[:3]
    rows, depth = source_latents.shape
    cols = target_latents.shape[0]
    feats = depth // (n_x * n_y)
    row_groups, col_groups = rows // LANES, cols // LANES
    t_peers, z_peers = n_x * n_y - 1, n_z - 1
    vmem = pl.BlockSpec(memory_space=pltpu.VMEM)
    hbm = pl.BlockSpec(memory_space=pltpu.HBM)
    anywhere = pl.BlockSpec(memory_space=pl.ANY)
    dma = pltpu.SemaphoreType.DMA
    chunk, half, band = rows // CHUNKS, feats // 2, n_y * feats // 2
    shapes = (
        jax.ShapeDtypeStruct((feats, rows), BF16),
        jax.ShapeDtypeStruct((row_groups, LANES), F32),
        jax.ShapeDtypeStruct((col_groups, LANES), F32),
    )
    results = pl.pallas_call(
        functools.partial(kernel, cfg),
        out_shape=shapes,
        in_specs=[hbm, hbm],
        out_specs=(vmem, vmem, vmem),
        scratch_shapes=[
            pltpu.VMEM((rows, depth), BF16),
            pltpu.VMEM((cols, depth), BF16),
            pltpu.VMEM((depth, cols), BF16),
            pltpu.VMEM((rows, cols), F32),
            pltpu.VMEM((rows, LANES), F32),
            pltpu.VMEM((rows, LANES), F32),
            pltpu.VMEM((rows, LANES), F32),
            pltpu.VMEM((rows, cols), BF16),
            pltpu.VMEM((CHUNKS, depth, chunk), BF16),
            pltpu.VMEM((CHUNKS, 2, n_x - 1, band, chunk), BF16),
            pltpu.VMEM((CHUNKS, 2, band, chunk), BF16),
            pltpu.VMEM((CHUNKS, 2, n_x - 1, half, chunk), BF16),
            pltpu.VMEM((col_groups, LANES), F32),
            pltpu.VMEM((row_groups, LANES), F32),
            pltpu.VMEM((row_groups, LANES), F32),
            pltpu.VMEM((col_groups, LANES), F32),
            pltpu.VMEM((col_groups * 8, LANES), F32),
            pltpu.VMEM((col_groups * 8, LANES), F32),
            pltpu.VMEM((row_groups, LANES), F32),
            pltpu.VMEM((ITERS + 1, row_groups, LANES), F32),
            pltpu.VMEM((ITERS + 1, t_peers, row_groups, LANES), F32),
            pltpu.VMEM((ITERS, col_groups, LANES), F32),
            pltpu.VMEM((ITERS, col_groups, LANES), F32),
            pltpu.VMEM((ITERS, col_groups, LANES), F32),
            pltpu.VMEM((ITERS, z_peers, col_groups, LANES), F32),
            dma((QUARTERS + 1,)),
            dma((ITERS + 1,)),
            dma((ITERS + 1,)),
            dma((ITERS,)),
            dma((ITERS,)),
            dma((ITERS,)),
            dma((ITERS,)),
            dma((CHUNKS,)),
            dma((CHUNKS,)),
            dma((CHUNKS,)),
            dma((CHUNKS,)),
        ],
        compiler_params=pltpu.CompilerParams(
            collective_id=0, has_side_effects=True, vmem_limit_bytes=213 << 18
        ),
        name="transport",
    )(source_latents, target_latents)
    moved, f, g = pl.pallas_call(
        hand_out,
        out_shape=shapes,
        in_specs=[anywhere] * 3,
        out_specs=(anywhere,) * 3,
        scratch_shapes=[dma((3,))],
        name="hand_out",
    )(*results)
    return moved.T, f.reshape(rows), g.reshape(cols)


def solution(mesh):
    n_src, n_tgt = mesh.shape["src"], mesh.shape["tgt"]
    n_x = math.isqrt(n_tgt)

    def whole(source_latents, target_latents):
        eps = 1.28 / math.sqrt(source_latents.shape[1])
        cfg = (
            n_src // 2,
            n_x,
            n_tgt // n_x,
            eps,
            math.log2(source_latents.shape[0]),
            math.log2(target_latents.shape[0]),
        )
        return jax.shard_map(
            functools.partial(local, cfg),
            mesh=mesh,
            in_specs=(P("src", None), P("tgt", None)),
            out_specs=(P("src", "tgt"), P("src"), P("tgt")),
            check_vma=False,
        )(source_latents, target_latents)

    return whole
```

```python
import functools
import math

import jax
import jax.numpy as jnp
from jax import lax
from jax.experimental import pallas as pl
from jax.experimental.pallas import tpu as pltpu
from jax.sharding import PartitionSpec as P

ITERS = 3
LOADS = 2
CHUNKS = 2
LOG2E = math.log2(math.e)
LANES = 128
F32 = jnp.float32
BF16 = jnp.bfloat16
NT_DIMS = (((1,), (1,)), ((), ()))


def ring_distance(k, n):
    return min(k, n - k)


def log2(x):
    return jnp.log(x) * LOG2E


def combine(parts):
    top = functools.reduce(jnp.maximum, parts)
    total = functools.reduce(jnp.add, [jnp.exp2(p - top) for p in parts])
    return top + log2(total)


def square_sums(block_ref, start, out_ref, row):
    width = block_ref.shape[1]
    total = jnp.zeros((LANES, LANES), F32)
    for c in range(width // LANES):
        piece = block_ref[pl.ds(start, LANES), c * LANES : (c + 1) * LANES].astype(F32)
        total = total + piece * piece
    out_ref[row : row + 1, :] = jnp.sum(total.T, axis=0, keepdims=True)


def kernel(
    cfg,
    src_hbm,
    tgt_hbm,
    moved_ref,
    f_ref,
    g_ref,
    a,
    b,
    b_t,
    scores,
    part,
    column,
    weights,
    sums,
    first_in,
    second_out,
    second_in,
    h_ref,
    u_ref,
    ss_ref,
    tt_ref,
    peak_ref,
    mass_ref,
    own_scale,
    t_send,
    t_recv,
    c_send,
    c_recv,
    z_send,
    z_recv,
    load_sem,
    t_ssem,
    t_rsem,
    c_ssem,
    c_rsem,
    z_ssem,
    z_rsem,
    m_ssem,
    m_rsem,
    n_ssem,
    n_rsem,
):
    n_z, n_x, n_y, eps, log2_rows, log2_cols = cfg
    rows, depth = a.shape
    cols = b.shape[0]
    row_groups, col_groups = rows // LANES, cols // LANES
    s_me, t_me = lax.axis_index("src"), lax.axis_index("tgt")
    z_me, core_me = s_me // 2, s_me % 2
    x_me, y_me = t_me // n_y, t_me % n_y
    half = depth // (n_x * n_y) // 2
    chunk = rows // CHUNKS

    z_peers = []
    for k in sorted(range(1, n_z), key=lambda k: -ring_distance(k, n_z)):
        z_peers.append({"src": ((z_me + k) % n_z) * 2 + core_me, "tgt": t_me})
    sibling = {"src": z_me * 2 + (1 - core_me), "tgt": t_me}
    steps = [(dx, dy) for dx in range(n_x) for dy in range(n_y) if dx or dy]
    steps.sort(key=lambda d: (-ring_distance(d[0], n_x), -ring_distance(d[1], n_y)))
    t_index = [((x_me + dx) % n_x) * n_y + (y_me + dy) % n_y for dx, dy in steps]
    far = sorted(
        range(len(steps)),
        key=lambda k: -ring_distance(steps[k][0], n_x) - ring_distance(steps[k][1], n_y),
    )

    barrier = pltpu.get_barrier_semaphore()
    everyone = z_peers + [{"src": s_me, "tgt": t_index[k]} for k in far] + [sibling]
    for peer in everyone:
        pl.semaphore_signal(
            barrier, inc=1, device_id=peer, device_id_type=pl.DeviceIdType.MESH
        )

    share = cols // LOADS
    loads = [pltpu.make_async_copy(src_hbm, a, load_sem.at[LOADS])]
    for q in range(LOADS):
        piece = pl.ds(q * share, share)
        loads.append(pltpu.make_async_copy(tgt_hbm.at[piece], b.at[piece], load_sem.at[q]))
    for copy in loads:
        copy.start()
    for q in range(LOADS):
        loads[1 + q].wait()
        blocks = range(q * share // LANES, (q + 1) * share // LANES)
        for c in blocks:
            square_sums(b, c * LANES, tt_ref, c)
        if q == 0:
            loads[0].wait()
        dot = lax.dot_general(
            a[...],
            b[q * share : (q + 1) * share, :],
            NT_DIMS,
            preferred_element_type=F32,
        )
        scores[:, q * share : (q + 1) * share] = dot * (2.0 * LOG2E / (depth * eps))
    h_ref[...] = tt_ref[...] * (-LOG2E / (depth * eps))

    def rows_pass(out_ref):
        shift = [
            jnp.broadcast_to(h_ref[c : c + 1, :], (8, LANES)) for c in range(col_groups)
        ]

        for k in range(0, rows, 8):
            v = [
                scores[k : k + 8, c * LANES : (c + 1) * LANES] + shift[c]
                for c in range(col_groups)
            ]
            part[k : k + 8, :] = combine(v)
        for r in range(row_groups):
            x = part[r * LANES : (r + 1) * LANES, :].T
            top = jnp.max(x, axis=0, keepdims=True)
            out_ref[r : r + 1, :] = top + log2(
                jnp.sum(jnp.exp2(x - top), axis=0, keepdims=True)
            )

    def to_column(ref):
        for r in range(row_groups):
            column[r * LANES : (r + 1) * LANES, :] = jnp.broadcast_to(
                ref[r : r + 1, :], (LANES, LANES)
            ).T

    def start_rows_exchange(i):
        for k in far:
            pltpu.make_async_remote_copy(
                src_ref=t_send.at[i],
                dst_ref=t_recv.at[i, k],
                send_sem=t_ssem.at[i],
                recv_sem=t_rsem.at[i],
                device_id={"src": s_me, "tgt": t_index[k]},
                device_id_type=pl.DeviceIdType.MESH,
            ).start()

    def wait_bytes(ref, sem):
        pltpu.make_async_copy(ref, ref, sem).wait()

    def columns_pass(out_ref):
        shape = (8, LANES)
        low = jnp.full(shape, -3.0e38, F32)
        start = tuple([low] * col_groups + [jnp.zeros(shape, F32)] * col_groups)

        def some_rows(block, carry):
            tops, totals = list(carry[:col_groups]), list(carry[col_groups:])
            at = [pl.ds(pl.multiple_of(block * 64 + k * 8, 8), 8) for k in range(8)]
            u = [column[p, :] for p in at]
            for c in range(col_groups):
                v = [scores[p, c * LANES : (c + 1) * LANES] + w for p, w in zip(at, u)]
                top = functools.reduce(jnp.maximum, v + [tops[c]])
                mass = functools.reduce(jnp.add, [jnp.exp2(p - top) for p in v])
                totals[c] = totals[c] * jnp.exp2(tops[c] - top) + mass
                tops[c] = top
            return tuple(tops + totals)

        done = lax.fori_loop(0, rows // 64, some_rows, start, unroll=4)
        for c in range(col_groups):
            peak_ref[c * 8 : (c + 1) * 8, :] = done[c]
            mass_ref[c * 8 : (c + 1) * 8, :] = done[col_groups + c]
        peaks = [peak_ref[pl.ds(r, col_groups, stride=8), :] for r in range(8)]
        masses = [mass_ref[pl.ds(r, col_groups, stride=8), :] for r in range(8)]
        top = functools.reduce(jnp.maximum, peaks)
        total = functools.reduce(
            jnp.add, [m * jnp.exp2(p - top) for p, m in zip(peaks, masses)]
        )
        out_ref[...] = top + log2(total)

    rows_pass(t_send.at[0])
    pl.semaphore_wait(barrier, len(everyone))
    start_rows_exchange(0)

    for r in range(row_groups):
        square_sums(a, r * LANES, ss_ref, r)
    order = sorted(range(n_x), key=lambda d: -ring_distance(d, n_x))

    def position(along):
        return sum(jnp.where(along == e, o, 0) for o, e in enumerate(order))

    def turn(block, carry):
        at = pl.ds(pl.multiple_of(block * LANES, LANES), LANES)
        for c in range(depth // LANES):
            turned = b[at, c * LANES : (c + 1) * LANES].T
            for o in range(LANES // half):
                owner, second = divmod(c * (LANES // half) + o, 2)
                ox, oy = owner // n_y, owner % n_y
                if second:
                    row = position((oy - y_me + n_y) % n_y) * (2 * n_y) + n_y + ox
                else:
                    row = position((ox - x_me + n_x) % n_x) * (2 * n_y) + oy
                b_t[pl.ds(pl.multiple_of(row * half, half), half), at] = turned[
                    o * half : (o + 1) * half
                ]
        return carry

    lax.fori_loop(0, col_groups, turn, 0)

    def sweep(i, carry):
        wait_bytes(t_recv.at[i], t_rsem.at[i])
        u_ref[...] = -log2_cols - combine(
            [t_send[i]] + [t_recv[i, k] for k in range(len(steps))]
        )
        to_column(u_ref)
        columns_pass(c_send.at[i])
        copy = pltpu.make_async_remote_copy(
            src_ref=c_send.at[i],
            dst_ref=c_recv.at[i],
            send_sem=c_ssem.at[i],
            recv_sem=c_rsem.at[i],
            device_id=sibling,
            device_id_type=pl.DeviceIdType.MESH,
        )
        copy.start()
        copy.wait_recv()
        z_send[i] = combine([c_send[i], c_recv[i]])
        for k, peer in enumerate(z_peers):
            pltpu.make_async_remote_copy(
                src_ref=z_send.at[i],
                dst_ref=z_recv.at[i, k],
                send_sem=z_ssem.at[i],
                recv_sem=z_rsem.at[i],
                device_id=peer,
                device_id_type=pl.DeviceIdType.MESH,
            ).start()
        wait_bytes(z_recv.at[i], z_rsem.at[i])
        h_ref[...] = -log2_rows - combine(
            [z_send[i]] + [z_recv[i, k] for k in range(len(z_peers))]
        )
        rows_pass(t_send.at[i + 1])
        start_rows_exchange(i + 1)
        return carry

    lax.fori_loop(0, ITERS, sweep, 0)

    to_column(t_send.at[ITERS])
    shift = [
        jnp.broadcast_to(h_ref[c : c + 1, :], (16, LANES)) for c in range(col_groups)
    ]

    def weigh(begin, end):
        for k in range(begin, end, 16):
            at = slice(k, k + 16)
            level = column[at, :]
            for c in range(col_groups):
                v = scores[at, c * LANES : (c + 1) * LANES] + shift[c]
                weights[at, c * LANES : (c + 1) * LANES] = jnp.exp2(v - level).astype(BF16)

    band = n_y * half

    def plane_peer(kind, step):
        if kind == 0:
            return {"src": s_me, "tgt": ((x_me + step) % n_x) * n_y + y_me}
        return {"src": s_me, "tgt": x_me * n_y + (y_me + step) % n_y}

    for n in range(CHUNKS):
        weigh(n * chunk, (n + 1) * chunk)
        for o in range(0, n_x, 2):
            at = pl.ds(o * 2 * band, 4 * band)
            dot = lax.dot_general(
                b_t[at, :],
                weights[n * chunk : (n + 1) * chunk, :],
                NT_DIMS,
                preferred_element_type=F32,
            )
            sums[n, at, :] = dot.astype(BF16)
            for p in (o, o + 1):
                for kind in range(2):
                    if order[p]:
                        pltpu.make_async_remote_copy(
                            src_ref=sums.at[n, pl.ds((2 * p + kind) * band, band)],
                            dst_ref=first_in.at[n, kind, order[p] - 1],
                            send_sem=m_ssem.at[n],
                            recv_sem=m_rsem.at[n],
                            device_id=plane_peer(kind, order[p]),
                            device_id_type=pl.DeviceIdType.MESH,
                        ).start()

    f_ref[...] = ss_ref[...] * (1.0 / depth) + u_ref[...] * (eps / LOG2E)
    g_ref[...] = tt_ref[...] * (1.0 / depth) + h_ref[...] * (eps / LOG2E)

    wait_bytes(t_recv.at[ITERS], t_rsem.at[ITERS])
    level = combine([t_send[ITERS]] + [t_recv[ITERS, k] for k in range(len(steps))])
    own_scale[...] = jnp.exp2(t_send[ITERS] - level)
    along = [[steps.index((d, 0)) for d in range(1, n_x)], [steps.index((0, d)) for d in range(1, n_y)]]
    for line in along:
        for k in line:
            t_recv[ITERS, k] = jnp.exp2(t_recv[ITERS, k] - level)

    own = order.index(0)
    lanes = [slice(r * LANES, (r + 1) * LANES) for r in range(chunk // LANES)]
    for n in range(CHUNKS):
        wait_bytes(first_in.at[n], m_rsem.at[n])
        for kind in range(2):
            for r, lane in enumerate(lanes):
                g = n * (chunk // LANES) + r
                at = pl.ds((2 * own + kind) * band, band)
                total = sums[n, at, lane].astype(F32) * own_scale[g : g + 1, :]
                for j, k in enumerate(along[kind]):
                    total += first_in[n, kind, j, :, lane].astype(F32) * t_recv[ITERS, k, g : g + 1, :]
                second_out[n, kind, :, lane] = total.astype(BF16)
            for step in order:
                if step:
                    to = (y_me + step) % n_y if kind == 0 else (x_me + step) % n_x
                    pltpu.make_async_remote_copy(
                        src_ref=second_out.at[n, kind, pl.ds(pl.multiple_of(to * half, half), half)],
                        dst_ref=second_in.at[n, kind, step - 1],
                        send_sem=n_ssem.at[n],
                        recv_sem=n_rsem.at[n],
                        device_id=plane_peer(1 - kind, step),
                        device_id_type=pl.DeviceIdType.MESH,
                    ).start()
    for n in range(CHUNKS):
        wait_bytes(second_in.at[n], n_rsem.at[n])
        for kind in range(2):
            me = y_me if kind == 0 else x_me
            mine = pl.ds(pl.multiple_of(me * half, half), half)
            for r, lane in enumerate(lanes):
                total = second_out[n, kind, mine, lane].astype(F32)
                for j in range(n_x - 1):
                    total += second_in[n, kind, j, :, lane].astype(F32)
                at = n * chunk + r * LANES
                moved_ref[kind * half : (kind + 1) * half, at : at + LANES] = total.astype(BF16)

    for i in range(ITERS):
        wait_bytes(c_send.at[i], c_ssem.at[i])
        wait_bytes(z_recv.at[i], z_ssem.at[i])
    for i in range(ITERS + 1):
        wait_bytes(t_recv.at[i], t_ssem.at[i])
    for n in range(CHUNKS):
        wait_bytes(first_in.at[n], m_ssem.at[n])
        wait_bytes(second_in.at[n], n_ssem.at[n])


def local(cfg, source_latents, target_latents):
    n_z, n_x, n_y = cfg[:3]
    rows, depth = source_latents.shape
    cols = target_latents.shape[0]
    feats = depth // (n_x * n_y)
    row_groups, col_groups = rows // LANES, cols // LANES
    t_peers, z_peers = n_x * n_y - 1, n_z - 1
    vmem = pl.BlockSpec(memory_space=pltpu.VMEM)
    hbm = pl.BlockSpec(memory_space=pltpu.HBM)
    dma = pltpu.SemaphoreType.DMA
    chunk, half, band = rows // CHUNKS, feats // 2, n_y * feats // 2
    shapes = (
        jax.ShapeDtypeStruct((feats, rows), BF16),
        jax.ShapeDtypeStruct((row_groups, LANES), F32),
        jax.ShapeDtypeStruct((col_groups, LANES), F32),
    )
    moved, f, g = pl.pallas_call(
        functools.partial(kernel, cfg),
        out_shape=shapes,
        in_specs=[hbm, hbm],
        out_specs=(vmem, vmem, vmem),
        scratch_shapes=[
            pltpu.VMEM((rows, depth), BF16),
            pltpu.VMEM((cols, depth), BF16),
            pltpu.VMEM((depth, cols), BF16),
            pltpu.VMEM((rows, cols), F32),
            pltpu.VMEM((rows, LANES), F32),
            pltpu.VMEM((rows, LANES), F32),
            pltpu.VMEM((rows, cols), BF16),
            pltpu.VMEM((CHUNKS, depth, chunk), BF16),
            pltpu.VMEM((CHUNKS, 2, n_x - 1, band, chunk), BF16),
            pltpu.VMEM((CHUNKS, 2, band, chunk), BF16),
            pltpu.VMEM((CHUNKS, 2, n_x - 1, half, chunk), BF16),
            pltpu.VMEM((col_groups, LANES), F32),
            pltpu.VMEM((row_groups, LANES), F32),
            pltpu.VMEM((row_groups, LANES), F32),
            pltpu.VMEM((col_groups, LANES), F32),
            pltpu.VMEM((col_groups * 8, LANES), F32),
            pltpu.VMEM((col_groups * 8, LANES), F32),
            pltpu.VMEM((row_groups, LANES), F32),
            pltpu.VMEM((ITERS + 1, row_groups, LANES), F32),
            pltpu.VMEM((ITERS + 1, t_peers, row_groups, LANES), F32),
            pltpu.VMEM((ITERS, col_groups, LANES), F32),
            pltpu.VMEM((ITERS, col_groups, LANES), F32),
            pltpu.VMEM((ITERS, col_groups, LANES), F32),
            pltpu.VMEM((ITERS, z_peers, col_groups, LANES), F32),
            dma((LOADS + 1,)),
            dma((ITERS + 1,)),
            dma((ITERS + 1,)),
            dma((ITERS,)),
            dma((ITERS,)),
            dma((ITERS,)),
            dma((ITERS,)),
            dma((CHUNKS,)),
            dma((CHUNKS,)),
            dma((CHUNKS,)),
            dma((CHUNKS,)),
        ],
        compiler_params=pltpu.CompilerParams(
            collective_id=0, has_side_effects=True, vmem_limit_bytes=213 << 18
        ),
        name="transport",
    )(source_latents, target_latents)
    return moved.T, f.reshape(rows), g.reshape(cols)


def solution(mesh):
    n_src, n_tgt = mesh.shape["src"], mesh.shape["tgt"]
    n_x = math.isqrt(n_tgt)

    def whole(source_latents, target_latents):
        eps = 1.28 / math.sqrt(source_latents.shape[1])
        cfg = (
            n_src // 2,
            n_x,
            n_tgt // n_x,
            eps,
            math.log2(source_latents.shape[0]),
            math.log2(target_latents.shape[0]),
        )
        return jax.shard_map(
            functools.partial(local, cfg),
            mesh=mesh,
            in_specs=(P("src", None), P("tgt", None)),
            out_specs=(P("src", "tgt"), P("src"), P("tgt")),
            check_vma=False,
        )(source_latents, target_latents)

    return whole
```

```python
import functools
import math

import jax
import jax.numpy as jnp
from jax import lax
from jax.experimental import pallas as pl
from jax.experimental.pallas import tpu as pltpu
from jax.sharding import PartitionSpec as P

ITERS = 3
LOADS = 2
CHUNKS = 2
LEAD = 0
LOG2E = math.log2(math.e)
LANES = 128
F32 = jnp.float32
BF16 = jnp.bfloat16
NT_DIMS = (((1,), (1,)), ((), ()))


def ring_distance(k, n):
    return min(k, n - k)


def log2(x):
    return jnp.log(x) * LOG2E


def tree(op, parts):
    while len(parts) > 1:
        paired = [op(p, q) for p, q in zip(parts[::2], parts[1::2])]
        parts = paired + parts[len(parts) - len(parts) % 2 :]
    return parts[0]


def combine(parts):
    top = tree(jnp.maximum, parts)
    return top + log2(tree(jnp.add, [jnp.exp2(p - top) for p in parts]))


def square_sums(block_ref, start, out_ref, row):
    width = block_ref.shape[1]
    total = jnp.zeros((LANES, LANES), F32)
    for c in range(width // LANES):
        piece = block_ref[pl.ds(start, LANES), c * LANES : (c + 1) * LANES].astype(F32)
        total = total + piece * piece
    out_ref[row : row + 1, :] = jnp.sum(total.T, axis=0, keepdims=True)


def kernel(
    cfg,
    src_hbm,
    tgt_hbm,
    moved_ref,
    f_ref,
    g_ref,
    a,
    b,
    b_t,
    scores,
    part,
    column,
    weights,
    sums,
    first_in,
    second_out,
    second_in,
    h_ref,
    u_ref,
    ss_ref,
    tt_ref,
    peak_ref,
    mass_ref,
    own_scale,
    t_send,
    t_recv,
    c_send,
    c_recv,
    z_recv,
    load_sem,
    t_ssem,
    t_rsem,
    c_ssem,
    c_rsem,
    z_ssem,
    z_rsem,
    m_ssem,
    m_rsem,
    n_ssem,
    n_rsem,
):
    n_z, n_x, n_y, eps, log2_rows, log2_cols = cfg
    rows, depth = a.shape
    cols = b.shape[0]
    row_groups, col_groups = rows // LANES, cols // LANES
    s_me, t_me = lax.axis_index("src"), lax.axis_index("tgt")
    z_me, core_me = s_me // 2, s_me % 2
    x_me, y_me = t_me // n_y, t_me % n_y
    half = depth // (n_x * n_y) // 2
    chunk = rows // CHUNKS

    z_steps = sorted(range(1, n_z), key=lambda k: -ring_distance(k, n_z))

    def z_peer(k, core):
        return {"src": ((z_me + k) % n_z) * 2 + core, "tgt": t_me}

    sibling = {"src": z_me * 2 + (1 - core_me), "tgt": t_me}
    steps = [(dx, dy) for dx in range(n_x) for dy in range(n_y) if dx or dy]
    steps.sort(key=lambda d: (-ring_distance(d[0], n_x), -ring_distance(d[1], n_y)))
    t_index = [((x_me + dx) % n_x) * n_y + (y_me + dy) % n_y for dx, dy in steps]
    far = sorted(
        range(len(steps)),
        key=lambda k: -ring_distance(steps[k][0], n_x) - ring_distance(steps[k][1], n_y),
    )

    share = cols // LOADS
    loads = [pltpu.make_async_copy(src_hbm, a, load_sem.at[LOADS])]
    for q in range(LOADS):
        piece = pl.ds(q * share, share)
        loads.append(pltpu.make_async_copy(tgt_hbm.at[piece], b.at[piece], load_sem.at[q]))
    for copy in loads:
        copy.start()

    leads = core_me == LEAD
    barrier = pltpu.get_barrier_semaphore()
    everyone = [z_peer(k, LEAD) for k in z_steps]
    everyone += [{"src": s_me, "tgt": t_index[k]} for k in far] + [sibling]
    for peer in everyone:
        pl.semaphore_signal(
            barrier, inc=1, device_id=peer, device_id_type=pl.DeviceIdType.MESH
        )

    for q in range(LOADS):
        loads[1 + q].wait()
        blocks = range(q * share // LANES, (q + 1) * share // LANES)
        for c in blocks:
            square_sums(b, c * LANES, tt_ref, c)
        if q == 0:
            loads[0].wait()
        dot = lax.dot_general(
            a[...],
            b[q * share : (q + 1) * share, :],
            NT_DIMS,
            preferred_element_type=F32,
        )
        scores[:, q * share : (q + 1) * share] = dot * (2.0 * LOG2E / (depth * eps))
    h_ref[...] = tt_ref[...] * (-LOG2E / (depth * eps))

    def rows_pass(out_ref):
        shift = [
            jnp.broadcast_to(h_ref[c : c + 1, :], (8, LANES)) for c in range(col_groups)
        ]

        for k in range(0, rows, 8):
            v = [
                scores[k : k + 8, c * LANES : (c + 1) * LANES] + shift[c]
                for c in range(col_groups)
            ]
            part[k : k + 8, :] = combine(v)
        for r in range(row_groups):
            x = part[r * LANES : (r + 1) * LANES, :].T
            top = jnp.max(x, axis=0, keepdims=True)
            out_ref[r : r + 1, :] = top + log2(
                jnp.sum(jnp.exp2(x - top), axis=0, keepdims=True)
            )

    def to_column(ref):
        for r in range(row_groups):
            column[r * LANES : (r + 1) * LANES, :] = jnp.broadcast_to(
                ref[r : r + 1, :], (LANES, LANES)
            ).T

    def start_rows_exchange(i):
        for k in far:
            pltpu.make_async_remote_copy(
                src_ref=t_send.at[i],
                dst_ref=t_recv.at[i, k],
                send_sem=t_ssem.at[i],
                recv_sem=t_rsem.at[i],
                device_id={"src": s_me, "tgt": t_index[k]},
                device_id_type=pl.DeviceIdType.MESH,
            ).start()

    def wait_bytes(ref, sem):
        pltpu.make_async_copy(ref, ref, sem).wait()

    def columns_pass(out_ref):
        shape = (8, LANES)
        low = jnp.full(shape, -3.0e38, F32)
        start = tuple([low] * col_groups + [jnp.zeros(shape, F32)] * col_groups)

        def some_rows(block, carry):
            tops, totals = list(carry[:col_groups]), list(carry[col_groups:])
            at = [pl.ds(pl.multiple_of(block * 64 + k * 8, 8), 8) for k in range(8)]
            u = [column[p, :] for p in at]
            for c in range(col_groups):
                v = [scores[p, c * LANES : (c + 1) * LANES] + w for p, w in zip(at, u)]
                top = jnp.maximum(tree(jnp.maximum, v), tops[c])
                mass = tree(jnp.add, [jnp.exp2(p - top) for p in v])
                totals[c] = totals[c] * jnp.exp2(tops[c] - top) + mass
                tops[c] = top
            return tuple(tops + totals)

        done = lax.fori_loop(0, rows // 64, some_rows, start, unroll=4)
        for c in range(col_groups):
            peak_ref[c * 8 : (c + 1) * 8, :] = done[c]
            mass_ref[c * 8 : (c + 1) * 8, :] = done[col_groups + c]
        peaks = [peak_ref[pl.ds(r, col_groups, stride=8), :] for r in range(8)]
        masses = [mass_ref[pl.ds(r, col_groups, stride=8), :] for r in range(8)]
        top = tree(jnp.maximum, peaks)
        total = tree(jnp.add, [m * jnp.exp2(p - top) for p, m in zip(peaks, masses)])
        out_ref[...] = top + log2(total)

    rows_pass(t_send.at[0])

    @pl.when(leads)
    def _():
        pl.semaphore_wait(barrier, len(far) + 1 + 2 * len(z_steps))

    @pl.when(jnp.logical_not(leads))
    def _():
        pl.semaphore_wait(barrier, len(far) + 1)

    start_rows_exchange(0)

    for r in range(row_groups):
        square_sums(a, r * LANES, ss_ref, r)
    order = sorted(range(n_x), key=lambda d: -ring_distance(d, n_x))

    def position(along):
        return sum(jnp.where(along == e, o, 0) for o, e in enumerate(order))

    def turn(block, carry):
        at = pl.ds(pl.multiple_of(block * LANES, LANES), LANES)
        for c in range(depth // LANES):
            turned = b[at, c * LANES : (c + 1) * LANES].T
            for o in range(LANES // half):
                owner, second = divmod(c * (LANES // half) + o, 2)
                ox, oy = owner // n_y, owner % n_y
                if second:
                    row = position((oy - y_me + n_y) % n_y) * (2 * n_y) + n_y + ox
                else:
                    row = position((ox - x_me + n_x) % n_x) * (2 * n_y) + oy
                b_t[pl.ds(pl.multiple_of(row * half, half), half), at] = turned[
                    o * half : (o + 1) * half
                ]
        return carry

    lax.fori_loop(0, col_groups, turn, 0)

    own_slot = n_z - 1

    def sweep(i, carry):
        wait_bytes(t_recv.at[i], t_rsem.at[i])
        u_ref[...] = -log2_cols - combine(
            [t_send[i]] + [t_recv[i, k] for k in range(len(steps))]
        )
        to_column(u_ref)
        columns_pass(c_send.at[i])
        copy = pltpu.make_async_remote_copy(
            src_ref=c_send.at[i],
            dst_ref=c_recv.at[i],
            send_sem=c_ssem.at[i],
            recv_sem=c_rsem.at[i],
            device_id=sibling,
            device_id_type=pl.DeviceIdType.MESH,
        )

        @pl.when(jnp.logical_not(leads))
        def _():
            copy.start()
            wait_bytes(z_recv.at[i], z_rsem.at[i])

        @pl.when(leads)
        def _():
            copy.wait_recv()
            z_recv[i, own_slot] = combine([c_send[i], c_recv[i]])

            def send(slot, peer):
                pltpu.make_async_remote_copy(
                    src_ref=z_recv.at[i, own_slot],
                    dst_ref=z_recv.at[i, slot],
                    send_sem=z_ssem.at[i],
                    recv_sem=z_rsem.at[i],
                    device_id=peer,
                    device_id_type=pl.DeviceIdType.MESH,
                ).start()

            for k in z_steps:
                send(k - 1, z_peer(k, 1 - LEAD))
                send(k - 1, z_peer(k, LEAD))
            send(own_slot, sibling)
            wait_bytes(z_recv.at[i, pl.ds(0, own_slot)], z_rsem.at[i])

        h_ref[...] = -log2_rows - combine([z_recv[i, k] for k in range(n_z)])
        rows_pass(t_send.at[i + 1])
        start_rows_exchange(i + 1)
        return carry

    lax.fori_loop(0, ITERS, sweep, 0)

    to_column(t_send.at[ITERS])
    shift = [
        jnp.broadcast_to(h_ref[c : c + 1, :], (16, LANES)) for c in range(col_groups)
    ]

    def weigh(begin, end):
        for k in range(begin, end, 16):
            at = slice(k, k + 16)
            level = column[at, :]
            for c in range(col_groups):
                v = scores[at, c * LANES : (c + 1) * LANES] + shift[c]
                weights[at, c * LANES : (c + 1) * LANES] = jnp.exp2(v - level).astype(BF16)

    band = n_y * half

    def plane_peer(kind, step):
        if kind == 0:
            return {"src": s_me, "tgt": ((x_me + step) % n_x) * n_y + y_me}
        return {"src": s_me, "tgt": x_me * n_y + (y_me + step) % n_y}

    for n in range(CHUNKS):
        weigh(n * chunk, (n + 1) * chunk)
        for o in range(0, n_x, 2):
            at = pl.ds(o * 2 * band, 4 * band)
            dot = lax.dot_general(
                b_t[at, :],
                weights[n * chunk : (n + 1) * chunk, :],
                NT_DIMS,
                preferred_element_type=F32,
            )
            sums[n, at, :] = dot.astype(BF16)
            for p in (o, o + 1):
                for kind in range(2):
                    if order[p]:
                        pltpu.make_async_remote_copy(
                            src_ref=sums.at[n, pl.ds((2 * p + kind) * band, band)],
                            dst_ref=first_in.at[n, kind, order[p] - 1],
                            send_sem=m_ssem.at[n],
                            recv_sem=m_rsem.at[n],
                            device_id=plane_peer(kind, order[p]),
                            device_id_type=pl.DeviceIdType.MESH,
                        ).start()

    f_ref[...] = ss_ref[...] * (1.0 / depth) + u_ref[...] * (eps / LOG2E)
    g_ref[...] = tt_ref[...] * (1.0 / depth) + h_ref[...] * (eps / LOG2E)

    wait_bytes(t_recv.at[ITERS], t_rsem.at[ITERS])
    level = combine([t_send[ITERS]] + [t_recv[ITERS, k] for k in range(len(steps))])
    own_scale[...] = jnp.exp2(t_send[ITERS] - level)
    along = [[steps.index((d, 0)) for d in range(1, n_x)], [steps.index((0, d)) for d in range(1, n_y)]]
    for line in along:
        for k in line:
            t_recv[ITERS, k] = jnp.exp2(t_recv[ITERS, k] - level)

    own = order.index(0)
    lanes = [slice(r * LANES, (r + 1) * LANES) for r in range(chunk // LANES)]
    for n in range(CHUNKS):
        wait_bytes(first_in.at[n], m_rsem.at[n])
        for kind in range(2):
            for r, lane in enumerate(lanes):
                g = n * (chunk // LANES) + r
                at = pl.ds((2 * own + kind) * band, band)
                total = sums[n, at, lane].astype(F32) * own_scale[g : g + 1, :]
                for j, k in enumerate(along[kind]):
                    total += first_in[n, kind, j, :, lane].astype(F32) * t_recv[ITERS, k, g : g + 1, :]
                second_out[n, kind, :, lane] = total.astype(BF16)
            for step in order:
                if step:
                    to = (y_me + step) % n_y if kind == 0 else (x_me + step) % n_x
                    pltpu.make_async_remote_copy(
                        src_ref=second_out.at[n, kind, pl.ds(pl.multiple_of(to * half, half), half)],
                        dst_ref=second_in.at[n, kind, step - 1],
                        send_sem=n_ssem.at[n],
                        recv_sem=n_rsem.at[n],
                        device_id=plane_peer(1 - kind, step),
                        device_id_type=pl.DeviceIdType.MESH,
                    ).start()
    for n in range(CHUNKS):
        wait_bytes(second_in.at[n], n_rsem.at[n])
        for kind in range(2):
            me = y_me if kind == 0 else x_me
            mine = pl.ds(pl.multiple_of(me * half, half), half)
            for r, lane in enumerate(lanes):
                total = second_out[n, kind, mine, lane].astype(F32)
                for j in range(n_x - 1):
                    total += second_in[n, kind, j, :, lane].astype(F32)
                at = n * chunk + r * LANES
                moved_ref[kind * half : (kind + 1) * half, at : at + LANES] = total.astype(BF16)

    for i in range(ITERS):

        @pl.when(jnp.logical_not(leads))
        def _():
            wait_bytes(c_send.at[i], c_ssem.at[i])

        @pl.when(leads)
        def _():
            wait_bytes(z_recv.at[i], z_ssem.at[i])
            wait_bytes(z_recv.at[i, pl.ds(0, own_slot)], z_ssem.at[i])

    for i in range(ITERS + 1):
        wait_bytes(t_recv.at[i], t_ssem.at[i])
    for n in range(CHUNKS):
        wait_bytes(first_in.at[n], m_ssem.at[n])
        wait_bytes(second_in.at[n], n_ssem.at[n])


def local(cfg, source_latents, target_latents):
    n_z, n_x, n_y = cfg[:3]
    rows, depth = source_latents.shape
    cols = target_latents.shape[0]
    feats = depth // (n_x * n_y)
    row_groups, col_groups = rows // LANES, cols // LANES
    t_peers = n_x * n_y - 1
    vmem = pl.BlockSpec(memory_space=pltpu.VMEM)
    hbm = pl.BlockSpec(memory_space=pltpu.HBM)
    dma = pltpu.SemaphoreType.DMA
    chunk, half, band = rows // CHUNKS, feats // 2, n_y * feats // 2
    shapes = (
        jax.ShapeDtypeStruct((feats, rows), BF16),
        jax.ShapeDtypeStruct((row_groups, LANES), F32),
        jax.ShapeDtypeStruct((col_groups, LANES), F32),
    )
    moved, f, g = pl.pallas_call(
        functools.partial(kernel, cfg),
        out_shape=shapes,
        in_specs=[hbm, hbm],
        out_specs=(vmem, vmem, vmem),
        scratch_shapes=[
            pltpu.VMEM((rows, depth), BF16),
            pltpu.VMEM((cols, depth), BF16),
            pltpu.VMEM((depth, cols), BF16),
            pltpu.VMEM((rows, cols), F32),
            pltpu.VMEM((rows, LANES), F32),
            pltpu.VMEM((rows, LANES), F32),
            pltpu.VMEM((rows, cols), BF16),
            pltpu.VMEM((CHUNKS, depth, chunk), BF16),
            pltpu.VMEM((CHUNKS, 2, n_x - 1, band, chunk), BF16),
            pltpu.VMEM((CHUNKS, 2, band, chunk), BF16),
            pltpu.VMEM((CHUNKS, 2, n_x - 1, half, chunk), BF16),
            pltpu.VMEM((col_groups, LANES), F32),
            pltpu.VMEM((row_groups, LANES), F32),
            pltpu.VMEM((row_groups, LANES), F32),
            pltpu.VMEM((col_groups, LANES), F32),
            pltpu.VMEM((col_groups * 8, LANES), F32),
            pltpu.VMEM((col_groups * 8, LANES), F32),
            pltpu.VMEM((row_groups, LANES), F32),
            pltpu.VMEM((ITERS + 1, row_groups, LANES), F32),
            pltpu.VMEM((ITERS + 1, t_peers, row_groups, LANES), F32),
            pltpu.VMEM((ITERS, col_groups, LANES), F32),
            pltpu.VMEM((ITERS, col_groups, LANES), F32),
            pltpu.VMEM((ITERS, n_z, col_groups, LANES), F32),
            dma((LOADS + 1,)),
            dma((ITERS + 1,)),
            dma((ITERS + 1,)),
            dma((ITERS,)),
            dma((ITERS,)),
            dma((ITERS,)),
            dma((ITERS,)),
            dma((CHUNKS,)),
            dma((CHUNKS,)),
            dma((CHUNKS,)),
            dma((CHUNKS,)),
        ],
        compiler_params=pltpu.CompilerParams(
            collective_id=0, has_side_effects=True, vmem_limit_bytes=213 << 18
        ),
        name="transport",
    )(source_latents, target_latents)
    return moved.T, f.reshape(rows), g.reshape(cols)


def solution(mesh):
    n_src, n_tgt = mesh.shape["src"], mesh.shape["tgt"]
    n_x = math.isqrt(n_tgt)

    def whole(source_latents, target_latents):
        eps = 1.28 / math.sqrt(source_latents.shape[1])
        cfg = (
            n_src // 2,
            n_x,
            n_tgt // n_x,
            eps,
            math.log2(source_latents.shape[0]),
            math.log2(target_latents.shape[0]),
        )
        return jax.shard_map(
            functools.partial(local, cfg),
            mesh=mesh,
            in_specs=(P("src", None), P("tgt", None)),
            out_specs=(P("src", "tgt"), P("src"), P("tgt")),
            check_vma=False,
        )(source_latents, target_latents)

    return whole
```

```python
import functools
import math

import jax
import jax.numpy as jnp
from jax import lax
from jax.experimental import pallas as pl
from jax.experimental.pallas import tpu as pltpu
from jax.sharding import PartitionSpec as P

ITERS = 3
LOADS = 2
CHUNKS = 2
LEAD = 0
LOG2E = math.log2(math.e)
LANES = 128
F32 = jnp.float32
BF16 = jnp.bfloat16
NT_DIMS = (((1,), (1,)), ((), ()))


def ring_distance(k, n):
    return min(k, n - k)


def log2(x):
    return jnp.log(x) * LOG2E


def tree(op, parts):
    while len(parts) > 1:
        paired = [op(p, q) for p, q in zip(parts[::2], parts[1::2])]
        parts = paired + parts[len(parts) - len(parts) % 2 :]
    return parts[0]


def combine(parts):
    top = tree(jnp.maximum, parts)
    return top + log2(tree(jnp.add, [jnp.exp2(p - top) for p in parts]))


def square_sums(block_ref, start, out_ref, row):
    width = block_ref.shape[1]
    total = jnp.zeros((LANES, LANES), F32)
    for c in range(width // LANES):
        piece = block_ref[pl.ds(start, LANES), c * LANES : (c + 1) * LANES].astype(F32)
        total = total + piece * piece
    out_ref[row : row + 1, :] = jnp.sum(total.T, axis=0, keepdims=True)


def kernel(
    cfg,
    src_hbm,
    tgt_hbm,
    moved_ref,
    f_ref,
    g_ref,
    a,
    b,
    b_t,
    scores,
    part,
    column,
    weights,
    sums,
    first_in,
    second_out,
    second_in,
    h_ref,
    u_ref,
    ss_ref,
    tt_ref,
    peak_ref,
    mass_ref,
    own_scale,
    t_send,
    t_recv,
    c_send,
    c_recv,
    z_recv,
    load_sem,
    t_ssem,
    t_rsem,
    c_ssem,
    c_rsem,
    z_ssem,
    z_rsem,
    m_ssem,
    m_rsem,
    n_ssem,
    n_rsem,
):
    n_z, n_x, n_y, eps, log2_rows, log2_cols = cfg
    rows, depth = a.shape
    cols = b.shape[0]
    row_groups, col_groups = rows // LANES, cols // LANES
    s_me, t_me = lax.axis_index("src"), lax.axis_index("tgt")
    z_me, core_me = s_me // 2, s_me % 2
    x_me, y_me = t_me // n_y, t_me % n_y
    half = depth // (n_x * n_y) // 2
    chunk = rows // CHUNKS

    z_steps = sorted(range(1, n_z), key=lambda k: -ring_distance(k, n_z))

    def z_peer(k, core):
        return {"src": ((z_me + k) % n_z) * 2 + core, "tgt": t_me}

    sibling = {"src": z_me * 2 + (1 - core_me), "tgt": t_me}
    steps = [(dx, dy) for dx in range(n_x) for dy in range(n_y) if dx or dy]
    steps.sort(key=lambda d: (-ring_distance(d[0], n_x), -ring_distance(d[1], n_y)))
    t_index = [((x_me + dx) % n_x) * n_y + (y_me + dy) % n_y for dx, dy in steps]
    far = sorted(
        range(len(steps)),
        key=lambda k: -ring_distance(steps[k][0], n_x) - ring_distance(steps[k][1], n_y),
    )

    share = cols // LOADS
    loads = [pltpu.make_async_copy(src_hbm, a, load_sem.at[LOADS])]
    for q in range(LOADS):
        piece = pl.ds(q * share, share)
        loads.append(pltpu.make_async_copy(tgt_hbm.at[piece], b.at[piece], load_sem.at[q]))
    for copy in loads:
        copy.start()

    leads = core_me == LEAD
    barrier = pltpu.get_barrier_semaphore()
    everyone = [z_peer(k, LEAD) for k in z_steps]
    everyone += [{"src": s_me, "tgt": t_index[k]} for k in far] + [sibling]
    for peer in everyone:
        pl.semaphore_signal(
            barrier, inc=1, device_id=peer, device_id_type=pl.DeviceIdType.MESH
        )

    for q in range(LOADS):
        loads[1 + q].wait()
        blocks = range(q * share // LANES, (q + 1) * share // LANES)
        for c in blocks:
            square_sums(b, c * LANES, tt_ref, c)
        if q == 0:
            loads[0].wait()
        dot = lax.dot_general(
            a[...],
            b[q * share : (q + 1) * share, :],
            NT_DIMS,
            preferred_element_type=F32,
        )
        scores[:, q * share : (q + 1) * share] = dot * (2.0 * LOG2E / (depth * eps))
    h_ref[...] = tt_ref[...] * (-LOG2E / (depth * eps))

    def rows_pass(out_ref, begin=0, end=rows):
        shift = [
            jnp.broadcast_to(h_ref[c : c + 1, :], (8, LANES)) for c in range(col_groups)
        ]

        for k in range(begin, end, 8):
            v = [
                scores[k : k + 8, c * LANES : (c + 1) * LANES] + shift[c]
                for c in range(col_groups)
            ]
            part[k : k + 8, :] = combine(v)
        for r in range(begin // LANES, end // LANES):
            x = part[r * LANES : (r + 1) * LANES, :].T
            top = jnp.max(x, axis=0, keepdims=True)
            out_ref[r : r + 1, :] = top + log2(
                jnp.sum(jnp.exp2(x - top), axis=0, keepdims=True)
            )

    def to_column(ref, begin=0, end=rows):
        for r in range(begin // LANES, end // LANES):
            column[r * LANES : (r + 1) * LANES, :] = jnp.broadcast_to(
                ref[r : r + 1, :], (LANES, LANES)
            ).T

    def start_rows_exchange(i):
        for k in far:
            pltpu.make_async_remote_copy(
                src_ref=t_send.at[i],
                dst_ref=t_recv.at[i, k],
                send_sem=t_ssem.at[i],
                recv_sem=t_rsem.at[i],
                device_id={"src": s_me, "tgt": t_index[k]},
                device_id_type=pl.DeviceIdType.MESH,
            ).start()

    def wait_bytes(ref, sem):
        pltpu.make_async_copy(ref, ref, sem).wait()

    def columns_pass(out_ref):
        shape = (8, LANES)
        low = jnp.full(shape, -3.0e38, F32)
        start = tuple([low] * col_groups + [jnp.zeros(shape, F32)] * col_groups)

        def some_rows(block, carry):
            tops, totals = list(carry[:col_groups]), list(carry[col_groups:])
            at = [pl.ds(pl.multiple_of(block * 64 + k * 8, 8), 8) for k in range(8)]
            u = [column[p, :] for p in at]
            for c in range(col_groups):
                v = [scores[p, c * LANES : (c + 1) * LANES] + w for p, w in zip(at, u)]
                top = jnp.maximum(tree(jnp.maximum, v), tops[c])
                mass = tree(jnp.add, [jnp.exp2(p - top) for p in v])
                totals[c] = totals[c] * jnp.exp2(tops[c] - top) + mass
                tops[c] = top
            return tuple(tops + totals)

        done = lax.fori_loop(0, rows // 64, some_rows, start, unroll=4)
        for c in range(col_groups):
            peak_ref[c * 8 : (c + 1) * 8, :] = done[c]
            mass_ref[c * 8 : (c + 1) * 8, :] = done[col_groups + c]
        peaks = [peak_ref[pl.ds(r, col_groups, stride=8), :] for r in range(8)]
        masses = [mass_ref[pl.ds(r, col_groups, stride=8), :] for r in range(8)]
        top = tree(jnp.maximum, peaks)
        total = tree(jnp.add, [m * jnp.exp2(p - top) for p, m in zip(peaks, masses)])
        out_ref[...] = top + log2(total)

    rows_pass(t_send.at[0])

    @pl.when(leads)
    def _():
        pl.semaphore_wait(barrier, len(far) + 1 + 2 * len(z_steps))

    @pl.when(jnp.logical_not(leads))
    def _():
        pl.semaphore_wait(barrier, len(far) + 1)

    start_rows_exchange(0)

    for r in range(row_groups):
        square_sums(a, r * LANES, ss_ref, r)
    order = sorted(range(n_x), key=lambda d: -ring_distance(d, n_x))

    def position(along):
        return sum(jnp.where(along == e, o, 0) for o, e in enumerate(order))

    def turn(block, carry):
        at = pl.ds(pl.multiple_of(block * LANES, LANES), LANES)
        for c in range(depth // LANES):
            turned = b[at, c * LANES : (c + 1) * LANES].T
            for o in range(LANES // half):
                owner, second = divmod(c * (LANES // half) + o, 2)
                ox, oy = owner // n_y, owner % n_y
                if second:
                    row = position((oy - y_me + n_y) % n_y) * (2 * n_y) + n_y + ox
                else:
                    row = position((ox - x_me + n_x) % n_x) * (2 * n_y) + oy
                b_t[pl.ds(pl.multiple_of(row * half, half), half), at] = turned[
                    o * half : (o + 1) * half
                ]
        return carry

    lax.fori_loop(0, col_groups, turn, 0)

    own_slot = n_z - 1

    def sweep(i, carry):
        wait_bytes(t_recv.at[i], t_rsem.at[i])
        u_ref[...] = -log2_cols - combine(
            [t_send[i]] + [t_recv[i, k] for k in range(len(steps))]
        )
        to_column(u_ref)
        columns_pass(c_send.at[i])
        copy = pltpu.make_async_remote_copy(
            src_ref=c_send.at[i],
            dst_ref=c_recv.at[i],
            send_sem=c_ssem.at[i],
            recv_sem=c_rsem.at[i],
            device_id=sibling,
            device_id_type=pl.DeviceIdType.MESH,
        )

        @pl.when(jnp.logical_not(leads))
        def _():
            copy.start()
            wait_bytes(z_recv.at[i], z_rsem.at[i])

        @pl.when(leads)
        def _():
            copy.wait_recv()
            z_recv[i, own_slot] = combine([c_send[i], c_recv[i]])

            def send(slot, peer):
                pltpu.make_async_remote_copy(
                    src_ref=z_recv.at[i, own_slot],
                    dst_ref=z_recv.at[i, slot],
                    send_sem=z_ssem.at[i],
                    recv_sem=z_rsem.at[i],
                    device_id=peer,
                    device_id_type=pl.DeviceIdType.MESH,
                ).start()

            for k in z_steps:
                send(k - 1, z_peer(k, 1 - LEAD))
                send(k - 1, z_peer(k, LEAD))
            send(own_slot, sibling)
            wait_bytes(z_recv.at[i, pl.ds(0, own_slot)], z_rsem.at[i])

        h_ref[...] = -log2_rows - combine([z_recv[i, k] for k in range(n_z)])

        @pl.when(i < ITERS - 1)
        def _():
            rows_pass(t_send.at[i + 1])
            start_rows_exchange(i + 1)

        return carry

    lax.fori_loop(0, ITERS, sweep, 0)

    shift = [
        jnp.broadcast_to(h_ref[c : c + 1, :], (16, LANES)) for c in range(col_groups)
    ]

    def weigh(begin, end):
        for k in range(begin, end, 16):
            at = slice(k, k + 16)
            level = column[at, :]
            for c in range(col_groups):
                v = scores[at, c * LANES : (c + 1) * LANES] + shift[c]
                weights[at, c * LANES : (c + 1) * LANES] = jnp.exp2(v - level).astype(BF16)

    band = n_y * half

    def plane_peer(kind, step):
        if kind == 0:
            return {"src": s_me, "tgt": ((x_me + step) % n_x) * n_y + y_me}
        return {"src": s_me, "tgt": x_me * n_y + (y_me + step) % n_y}

    for n in range(CHUNKS):
        rows_pass(t_send.at[ITERS], n * chunk, (n + 1) * chunk)
        if n == CHUNKS - 1:
            start_rows_exchange(ITERS)
        to_column(t_send.at[ITERS], n * chunk, (n + 1) * chunk)
        weigh(n * chunk, (n + 1) * chunk)
        for o in range(0, n_x, 2):
            at = pl.ds(o * 2 * band, 4 * band)
            dot = lax.dot_general(
                b_t[at, :],
                weights[n * chunk : (n + 1) * chunk, :],
                NT_DIMS,
                preferred_element_type=F32,
            )
            sums[n, at, :] = dot.astype(BF16)
            for p in (o, o + 1):
                for kind in range(2):
                    if order[p]:
                        pltpu.make_async_remote_copy(
                            src_ref=sums.at[n, pl.ds((2 * p + kind) * band, band)],
                            dst_ref=first_in.at[n, kind, order[p] - 1],
                            send_sem=m_ssem.at[n],
                            recv_sem=m_rsem.at[n],
                            device_id=plane_peer(kind, order[p]),
                            device_id_type=pl.DeviceIdType.MESH,
                        ).start()

    f_ref[...] = ss_ref[...] * (1.0 / depth) + u_ref[...] * (eps / LOG2E)
    g_ref[...] = tt_ref[...] * (1.0 / depth) + h_ref[...] * (eps / LOG2E)

    wait_bytes(t_recv.at[ITERS], t_rsem.at[ITERS])
    level = combine([t_send[ITERS]] + [t_recv[ITERS, k] for k in range(len(steps))])
    own_scale[...] = jnp.exp2(t_send[ITERS] - level)
    along = [[steps.index((d, 0)) for d in range(1, n_x)], [steps.index((0, d)) for d in range(1, n_y)]]
    for line in along:
        for k in line:
            t_recv[ITERS, k] = jnp.exp2(t_recv[ITERS, k] - level)

    own = order.index(0)
    lanes = [slice(r * LANES, (r + 1) * LANES) for r in range(chunk // LANES)]
    for n in range(CHUNKS):
        wait_bytes(first_in.at[n], m_rsem.at[n])
        for kind in range(2):
            for r, lane in enumerate(lanes):
                g = n * (chunk // LANES) + r
                at = pl.ds((2 * own + kind) * band, band)
                total = sums[n, at, lane].astype(F32) * own_scale[g : g + 1, :]
                for j, k in enumerate(along[kind]):
                    total += first_in[n, kind, j, :, lane].astype(F32) * t_recv[ITERS, k, g : g + 1, :]
                second_out[n, kind, :, lane] = total.astype(BF16)
            for step in order:
                if step:
                    to = (y_me + step) % n_y if kind == 0 else (x_me + step) % n_x
                    pltpu.make_async_remote_copy(
                        src_ref=second_out.at[n, kind, pl.ds(pl.multiple_of(to * half, half), half)],
                        dst_ref=second_in.at[n, kind, step - 1],
                        send_sem=n_ssem.at[n],
                        recv_sem=n_rsem.at[n],
                        device_id=plane_peer(1 - kind, step),
                        device_id_type=pl.DeviceIdType.MESH,
                    ).start()
    for n in range(CHUNKS):
        wait_bytes(second_in.at[n], n_rsem.at[n])
        for kind in range(2):
            me = y_me if kind == 0 else x_me
            mine = pl.ds(pl.multiple_of(me * half, half), half)
            for r, lane in enumerate(lanes):
                total = second_out[n, kind, mine, lane].astype(F32)
                for j in range(n_x - 1):
                    total += second_in[n, kind, j, :, lane].astype(F32)
                at = n * chunk + r * LANES
                moved_ref[kind * half : (kind + 1) * half, at : at + LANES] = total.astype(BF16)

    for i in range(ITERS):

        @pl.when(jnp.logical_not(leads))
        def _():
            wait_bytes(c_send.at[i], c_ssem.at[i])

        @pl.when(leads)
        def _():
            wait_bytes(z_recv.at[i], z_ssem.at[i])
            wait_bytes(z_recv.at[i, pl.ds(0, own_slot)], z_ssem.at[i])

    for i in range(ITERS + 1):
        wait_bytes(t_recv.at[i], t_ssem.at[i])
    for n in range(CHUNKS):
        wait_bytes(first_in.at[n], m_ssem.at[n])
        wait_bytes(second_in.at[n], n_ssem.at[n])


def local(cfg, source_latents, target_latents):
    n_z, n_x, n_y = cfg[:3]
    rows, depth = source_latents.shape
    cols = target_latents.shape[0]
    feats = depth // (n_x * n_y)
    row_groups, col_groups = rows // LANES, cols // LANES
    t_peers = n_x * n_y - 1
    vmem = pl.BlockSpec(memory_space=pltpu.VMEM)
    hbm = pl.BlockSpec(memory_space=pltpu.HBM)
    dma = pltpu.SemaphoreType.DMA
    chunk, half, band = rows // CHUNKS, feats // 2, n_y * feats // 2
    shapes = (
        jax.ShapeDtypeStruct((feats, rows), BF16),
        jax.ShapeDtypeStruct((row_groups, LANES), F32),
        jax.ShapeDtypeStruct((col_groups, LANES), F32),
    )
    moved, f, g = pl.pallas_call(
        functools.partial(kernel, cfg),
        out_shape=shapes,
        in_specs=[hbm, hbm],
        out_specs=(vmem, vmem, vmem),
        scratch_shapes=[
            pltpu.VMEM((rows, depth), BF16),
            pltpu.VMEM((cols, depth), BF16),
            pltpu.VMEM((depth, cols), BF16),
            pltpu.VMEM((rows, cols), F32),
            pltpu.VMEM((rows, LANES), F32),
            pltpu.VMEM((rows, LANES), F32),
            pltpu.VMEM((rows, cols), BF16),
            pltpu.VMEM((CHUNKS, depth, chunk), BF16),
            pltpu.VMEM((CHUNKS, 2, n_x - 1, band, chunk), BF16),
            pltpu.VMEM((CHUNKS, 2, band, chunk), BF16),
            pltpu.VMEM((CHUNKS, 2, n_x - 1, half, chunk), BF16),
            pltpu.VMEM((col_groups, LANES), F32),
            pltpu.VMEM((row_groups, LANES), F32),
            pltpu.VMEM((row_groups, LANES), F32),
            pltpu.VMEM((col_groups, LANES), F32),
            pltpu.VMEM((col_groups * 8, LANES), F32),
            pltpu.VMEM((col_groups * 8, LANES), F32),
            pltpu.VMEM((row_groups, LANES), F32),
            pltpu.VMEM((ITERS + 1, row_groups, LANES), F32),
            pltpu.VMEM((ITERS + 1, t_peers, row_groups, LANES), F32),
            pltpu.VMEM((ITERS, col_groups, LANES), F32),
            pltpu.VMEM((ITERS, col_groups, LANES), F32),
            pltpu.VMEM((ITERS, n_z, col_groups, LANES), F32),
            dma((LOADS + 1,)),
            dma((ITERS + 1,)),
            dma((ITERS + 1,)),
            dma((ITERS,)),
            dma((ITERS,)),
            dma((ITERS,)),
            dma((ITERS,)),
            dma((CHUNKS,)),
            dma((CHUNKS,)),
            dma((CHUNKS,)),
            dma((CHUNKS,)),
        ],
        compiler_params=pltpu.CompilerParams(
            collective_id=0, has_side_effects=True, vmem_limit_bytes=213 << 18
        ),
        name="transport",
    )(source_latents, target_latents)
    return moved.T, f.reshape(rows), g.reshape(cols)


def solution(mesh):
    n_src, n_tgt = mesh.shape["src"], mesh.shape["tgt"]
    n_x = math.isqrt(n_tgt)

    def whole(source_latents, target_latents):
        eps = 1.28 / math.sqrt(source_latents.shape[1])
        cfg = (
            n_src // 2,
            n_x,
            n_tgt // n_x,
            eps,
            math.log2(source_latents.shape[0]),
            math.log2(target_latents.shape[0]),
        )
        return jax.shard_map(
            functools.partial(local, cfg),
            mesh=mesh,
            in_specs=(P("src", None), P("tgt", None)),
            out_specs=(P("src", "tgt"), P("src"), P("tgt")),
            check_vma=False,
        )(source_latents, target_latents)

    return whole
```

```python
import functools
import math

import jax
import jax.numpy as jnp
from jax import lax
from jax.experimental import pallas as pl
from jax.experimental.pallas import tpu as pltpu
from jax.sharding import PartitionSpec as P

ITERS = 3
LOADS = 2
CHUNKS = 2
LEAD = 0
LOG2E = math.log2(math.e)
LANES = 128
F32 = jnp.float32
BF16 = jnp.bfloat16
NT_DIMS = (((1,), (1,)), ((), ()))


def ring_distance(k, n):
    return min(k, n - k)


def log2(x):
    return jnp.log(x) * LOG2E


def tree(op, parts):
    while len(parts) > 1:
        paired = [op(p, q) for p, q in zip(parts[::2], parts[1::2])]
        parts = paired + parts[len(parts) - len(parts) % 2 :]
    return parts[0]


def combine(parts):
    top = tree(jnp.maximum, parts)
    return top + log2(tree(jnp.add, [jnp.exp2(p - top) for p in parts]))


def square_sums(block_ref, start, out_ref, row):
    width = block_ref.shape[1]
    total = jnp.zeros((LANES, LANES), F32)
    for c in range(width // LANES):
        piece = block_ref[pl.ds(start, LANES), c * LANES : (c + 1) * LANES].astype(F32)
        total = total + piece * piece
    out_ref[row : row + 1, :] = jnp.sum(total.T, axis=0, keepdims=True)


def kernel(
    cfg,
    src_hbm,
    tgt_hbm,
    moved_ref,
    f_ref,
    g_ref,
    a,
    b,
    b_t,
    scores,
    part,
    column,
    weights,
    sums,
    first_in,
    second_out,
    second_in,
    h_ref,
    u_ref,
    ss_ref,
    tt_ref,
    peak_ref,
    mass_ref,
    own_scale,
    t_send,
    t_recv,
    c_send,
    c_recv,
    z_recv,
    load_sem,
    t_ssem,
    t_rsem,
    c_ssem,
    c_rsem,
    z_ssem,
    z_rsem,
    m_ssem,
    m_rsem,
    n_ssem,
    n_rsem,
):
    n_z, n_x, n_y, eps, log2_rows, log2_cols = cfg
    rows, depth = a.shape
    cols = b.shape[0]
    row_groups, col_groups = rows // LANES, cols // LANES
    s_me, t_me = lax.axis_index("src"), lax.axis_index("tgt")
    z_me, core_me = s_me // 2, s_me % 2
    x_me, y_me = t_me // n_y, t_me % n_y
    half = depth // (n_x * n_y) // 2
    chunk = rows // CHUNKS

    z_steps = sorted(range(1, n_z), key=lambda k: -ring_distance(k, n_z))

    def z_peer(k, core):
        return {"src": ((z_me + k) % n_z) * 2 + core, "tgt": t_me}

    sibling = {"src": z_me * 2 + (1 - core_me), "tgt": t_me}
    steps = [(dx, dy) for dx in range(n_x) for dy in range(n_y) if dx or dy]
    steps.sort(key=lambda d: (-ring_distance(d[0], n_x), -ring_distance(d[1], n_y)))
    t_index = [((x_me + dx) % n_x) * n_y + (y_me + dy) % n_y for dx, dy in steps]
    far = sorted(
        range(len(steps)),
        key=lambda k: -ring_distance(steps[k][0], n_x) - ring_distance(steps[k][1], n_y),
    )

    share = cols // LOADS
    loads = [pltpu.make_async_copy(src_hbm, a, load_sem.at[LOADS])]
    for q in range(LOADS):
        piece = pl.ds(q * share, share)
        loads.append(pltpu.make_async_copy(tgt_hbm.at[piece], b.at[piece], load_sem.at[q]))
    for copy in loads:
        copy.start()

    leads = core_me == LEAD
    barrier = pltpu.get_barrier_semaphore()
    everyone = [z_peer(k, LEAD) for k in z_steps]
    everyone += [{"src": s_me, "tgt": t_index[k]} for k in far] + [sibling]
    for peer in everyone:
        pl.semaphore_signal(
            barrier, inc=1, device_id=peer, device_id_type=pl.DeviceIdType.MESH
        )

    for q in range(LOADS):
        loads[1 + q].wait()
        blocks = range(q * share // LANES, (q + 1) * share // LANES)
        for c in blocks:
            square_sums(b, c * LANES, tt_ref, c)
        if q == 0:
            loads[0].wait()
        dot = lax.dot_general(
            a[...],
            b[q * share : (q + 1) * share, :],
            NT_DIMS,
            preferred_element_type=F32,
        )
        scores[:, q * share : (q + 1) * share] = dot * (2.0 * LOG2E / (depth * eps))
    h_ref[...] = tt_ref[...] * (-LOG2E / (depth * eps))

    groups = chunk // LANES

    def rows_pass(i, n):
        shift = [
            jnp.broadcast_to(h_ref[c : c + 1, :], (8, LANES)) for c in range(col_groups)
        ]

        for k in range(n * chunk, (n + 1) * chunk, 8):
            v = [
                scores[k : k + 8, c * LANES : (c + 1) * LANES] + shift[c]
                for c in range(col_groups)
            ]
            part[k : k + 8, :] = combine(v)
        for r in range(groups):
            at = n * chunk + r * LANES
            x = part[at : at + LANES, :].T
            top = jnp.max(x, axis=0, keepdims=True)
            t_send[i, n, r : r + 1, :] = top + log2(
                jnp.sum(jnp.exp2(x - top), axis=0, keepdims=True)
            )

    def to_column(ref, n):
        for r in range(groups):
            at = n * chunk + r * LANES
            column[at : at + LANES, :] = jnp.broadcast_to(
                ref[r : r + 1, :], (LANES, LANES)
            ).T

    def start_rows_exchange(i, n):
        for k in far:
            pltpu.make_async_remote_copy(
                src_ref=t_send.at[i, n],
                dst_ref=t_recv.at[i, n, k],
                send_sem=t_ssem.at[i, n],
                recv_sem=t_rsem.at[i, n],
                device_id={"src": s_me, "tgt": t_index[k]},
                device_id_type=pl.DeviceIdType.MESH,
            ).start()

    def wait_bytes(ref, sem):
        pltpu.make_async_copy(ref, ref, sem).wait()

    def columns_pass(i, out_ref):
        shape = (8, LANES)
        low = jnp.full(shape, -3.0e38, F32)
        start = tuple([low] * col_groups + [jnp.zeros(shape, F32)] * col_groups)

        def some_rows(block, carry):
            tops, totals = list(carry[:col_groups]), list(carry[col_groups:])
            at = [pl.ds(pl.multiple_of(block * 64 + k * 8, 8), 8) for k in range(8)]
            u = [column[p, :] for p in at]
            for c in range(col_groups):
                v = [scores[p, c * LANES : (c + 1) * LANES] + w for p, w in zip(at, u)]
                top = jnp.maximum(tree(jnp.maximum, v), tops[c])
                mass = tree(jnp.add, [jnp.exp2(p - top) for p in v])
                totals[c] = totals[c] * jnp.exp2(tops[c] - top) + mass
                tops[c] = top
            return tuple(tops + totals)

        done = start
        for n in range(CHUNKS):
            wait_bytes(t_recv.at[i, n], t_rsem.at[i, n])
            u_ref[n] = -log2_cols - combine(
                [t_send[i, n]] + [t_recv[i, n, k] for k in range(len(steps))]
            )
            to_column(u_ref.at[n], n)
            per = chunk // 64
            done = lax.fori_loop(n * per, (n + 1) * per, some_rows, done, unroll=True)
        for c in range(col_groups):
            peak_ref[c * 8 : (c + 1) * 8, :] = done[c]
            mass_ref[c * 8 : (c + 1) * 8, :] = done[col_groups + c]
        peaks = [peak_ref[pl.ds(r, col_groups, stride=8), :] for r in range(8)]
        masses = [mass_ref[pl.ds(r, col_groups, stride=8), :] for r in range(8)]
        top = tree(jnp.maximum, peaks)
        total = tree(jnp.add, [m * jnp.exp2(p - top) for p, m in zip(peaks, masses)])
        out_ref[...] = top + log2(total)

    rows_pass(0, 0)

    @pl.when(leads)
    def _():
        pl.semaphore_wait(barrier, len(far) + 1 + 2 * len(z_steps))

    @pl.when(jnp.logical_not(leads))
    def _():
        pl.semaphore_wait(barrier, len(far) + 1)

    start_rows_exchange(0, 0)
    for n in range(1, CHUNKS):
        rows_pass(0, n)
        start_rows_exchange(0, n)

    for r in range(row_groups):
        square_sums(a, r * LANES, ss_ref, r)
    order = sorted(range(n_x), key=lambda d: -ring_distance(d, n_x))

    def position(along):
        return sum(jnp.where(along == e, o, 0) for o, e in enumerate(order))

    def turn(block, carry):
        at = pl.ds(pl.multiple_of(block * LANES, LANES), LANES)
        for c in range(depth // LANES):
            turned = b[at, c * LANES : (c + 1) * LANES].T
            for o in range(LANES // half):
                owner, second = divmod(c * (LANES // half) + o, 2)
                ox, oy = owner // n_y, owner % n_y
                if second:
                    row = position((oy - y_me + n_y) % n_y) * (2 * n_y) + n_y + ox
                else:
                    row = position((ox - x_me + n_x) % n_x) * (2 * n_y) + oy
                b_t[pl.ds(pl.multiple_of(row * half, half), half), at] = turned[
                    o * half : (o + 1) * half
                ]
        return carry

    lax.fori_loop(0, col_groups, turn, 0)

    own_slot = n_z - 1

    def sweep(i, carry):
        columns_pass(i, c_send.at[i])
        copy = pltpu.make_async_remote_copy(
            src_ref=c_send.at[i],
            dst_ref=c_recv.at[i],
            send_sem=c_ssem.at[i],
            recv_sem=c_rsem.at[i],
            device_id=sibling,
            device_id_type=pl.DeviceIdType.MESH,
        )

        @pl.when(jnp.logical_not(leads))
        def _():
            copy.start()
            wait_bytes(z_recv.at[i], z_rsem.at[i])

        @pl.when(leads)
        def _():
            copy.wait_recv()
            z_recv[i, own_slot] = combine([c_send[i], c_recv[i]])

            def send(slot, peer):
                pltpu.make_async_remote_copy(
                    src_ref=z_recv.at[i, own_slot],
                    dst_ref=z_recv.at[i, slot],
                    send_sem=z_ssem.at[i],
                    recv_sem=z_rsem.at[i],
                    device_id=peer,
                    device_id_type=pl.DeviceIdType.MESH,
                ).start()

            for k in z_steps:
                send(k - 1, z_peer(k, 1 - LEAD))
                send(k - 1, z_peer(k, LEAD))
            send(own_slot, sibling)
            wait_bytes(z_recv.at[i, pl.ds(0, own_slot)], z_rsem.at[i])

        h_ref[...] = -log2_rows - combine([z_recv[i, k] for k in range(n_z)])

        @pl.when(i < ITERS - 1)
        def _():
            for n in range(CHUNKS):
                rows_pass(i + 1, n)
                start_rows_exchange(i + 1, n)

        return carry

    lax.fori_loop(0, ITERS, sweep, 0)

    shift = [
        jnp.broadcast_to(h_ref[c : c + 1, :], (16, LANES)) for c in range(col_groups)
    ]

    def weigh(begin, end):
        for k in range(begin, end, 16):
            at = slice(k, k + 16)
            level = column[at, :]
            for c in range(col_groups):
                v = scores[at, c * LANES : (c + 1) * LANES] + shift[c]
                weights[at, c * LANES : (c + 1) * LANES] = jnp.exp2(v - level).astype(BF16)

    band = n_y * half

    def plane_peer(kind, step):
        if kind == 0:
            return {"src": s_me, "tgt": ((x_me + step) % n_x) * n_y + y_me}
        return {"src": s_me, "tgt": x_me * n_y + (y_me + step) % n_y}

    for n in range(CHUNKS):
        rows_pass(ITERS, n)
        start_rows_exchange(ITERS, n)
        to_column(t_send.at[ITERS, n], n)
        weigh(n * chunk, (n + 1) * chunk)
        for o in range(0, n_x, 2):
            at = pl.ds(o * 2 * band, 4 * band)
            dot = lax.dot_general(
                b_t[at, :],
                weights[n * chunk : (n + 1) * chunk, :],
                NT_DIMS,
                preferred_element_type=F32,
            )
            sums[n, at, :] = dot.astype(BF16)
            for p in (o, o + 1):
                for kind in range(2):
                    if order[p]:
                        pltpu.make_async_remote_copy(
                            src_ref=sums.at[n, pl.ds((2 * p + kind) * band, band)],
                            dst_ref=first_in.at[n, kind, order[p] - 1],
                            send_sem=m_ssem.at[n],
                            recv_sem=m_rsem.at[n],
                            device_id=plane_peer(kind, order[p]),
                            device_id_type=pl.DeviceIdType.MESH,
                        ).start()

    for n in range(CHUNKS):
        at = slice(n * groups, (n + 1) * groups)
        f_ref[at, :] = ss_ref[at, :] * (1.0 / depth) + u_ref[n] * (eps / LOG2E)
    g_ref[...] = tt_ref[...] * (1.0 / depth) + h_ref[...] * (eps / LOG2E)

    along = [
        [steps.index((d, 0)) for d in range(1, n_x)],
        [steps.index((0, d)) for d in range(1, n_y)],
    ]
    for n in range(CHUNKS):
        wait_bytes(t_recv.at[ITERS, n], t_rsem.at[ITERS, n])
        level = combine(
            [t_send[ITERS, n]] + [t_recv[ITERS, n, k] for k in range(len(steps))]
        )
        own_scale[n] = jnp.exp2(t_send[ITERS, n] - level)
        for line in along:
            for k in line:
                t_recv[ITERS, n, k] = jnp.exp2(t_recv[ITERS, n, k] - level)

    own = order.index(0)
    lanes = [slice(r * LANES, (r + 1) * LANES) for r in range(chunk // LANES)]
    for n in range(CHUNKS):
        wait_bytes(first_in.at[n], m_rsem.at[n])
        for kind in range(2):
            for r, lane in enumerate(lanes):
                at = pl.ds((2 * own + kind) * band, band)
                total = sums[n, at, lane].astype(F32) * own_scale[n, r : r + 1, :]
                for j, k in enumerate(along[kind]):
                    total += first_in[n, kind, j, :, lane].astype(F32) * t_recv[ITERS, n, k, r : r + 1, :]
                second_out[n, kind, :, lane] = total.astype(BF16)
            for step in order:
                if step:
                    to = (y_me + step) % n_y if kind == 0 else (x_me + step) % n_x
                    pltpu.make_async_remote_copy(
                        src_ref=second_out.at[n, kind, pl.ds(pl.multiple_of(to * half, half), half)],
                        dst_ref=second_in.at[n, kind, step - 1],
                        send_sem=n_ssem.at[n],
                        recv_sem=n_rsem.at[n],
                        device_id=plane_peer(1 - kind, step),
                        device_id_type=pl.DeviceIdType.MESH,
                    ).start()
    for n in range(CHUNKS):
        wait_bytes(second_in.at[n], n_rsem.at[n])
        for kind in range(2):
            me = y_me if kind == 0 else x_me
            mine = pl.ds(pl.multiple_of(me * half, half), half)
            for r, lane in enumerate(lanes):
                total = second_out[n, kind, mine, lane].astype(F32)
                for j in range(n_x - 1):
                    total += second_in[n, kind, j, :, lane].astype(F32)
                at = n * chunk + r * LANES
                moved_ref[kind * half : (kind + 1) * half, at : at + LANES] = total.astype(BF16)

    for i in range(ITERS):

        @pl.when(jnp.logical_not(leads))
        def _():
            wait_bytes(c_send.at[i], c_ssem.at[i])

        @pl.when(leads)
        def _():
            wait_bytes(z_recv.at[i], z_ssem.at[i])
            wait_bytes(z_recv.at[i, pl.ds(0, own_slot)], z_ssem.at[i])

    for i in range(ITERS + 1):
        for n in range(CHUNKS):
            wait_bytes(t_recv.at[i, n], t_ssem.at[i, n])
    for n in range(CHUNKS):
        wait_bytes(first_in.at[n], m_ssem.at[n])
        wait_bytes(second_in.at[n], n_ssem.at[n])


def local(cfg, source_latents, target_latents):
    n_z, n_x, n_y = cfg[:3]
    rows, depth = source_latents.shape
    cols = target_latents.shape[0]
    feats = depth // (n_x * n_y)
    row_groups, col_groups = rows // LANES, cols // LANES
    groups = rows // CHUNKS // LANES
    t_peers = n_x * n_y - 1
    vmem = pl.BlockSpec(memory_space=pltpu.VMEM)
    hbm = pl.BlockSpec(memory_space=pltpu.HBM)
    dma = pltpu.SemaphoreType.DMA
    chunk, half, band = rows // CHUNKS, feats // 2, n_y * feats // 2
    shapes = (
        jax.ShapeDtypeStruct((feats, rows), BF16),
        jax.ShapeDtypeStruct((row_groups, LANES), F32),
        jax.ShapeDtypeStruct((col_groups, LANES), F32),
    )
    moved, f, g = pl.pallas_call(
        functools.partial(kernel, cfg),
        out_shape=shapes,
        in_specs=[hbm, hbm],
        out_specs=(vmem, vmem, vmem),
        scratch_shapes=[
            pltpu.VMEM((rows, depth), BF16),
            pltpu.VMEM((cols, depth), BF16),
            pltpu.VMEM((depth, cols), BF16),
            pltpu.VMEM((rows, cols), F32),
            pltpu.VMEM((rows, LANES), F32),
            pltpu.VMEM((rows, LANES), F32),
            pltpu.VMEM((rows, cols), BF16),
            pltpu.VMEM((CHUNKS, depth, chunk), BF16),
            pltpu.VMEM((CHUNKS, 2, n_x - 1, band, chunk), BF16),
            pltpu.VMEM((CHUNKS, 2, band, chunk), BF16),
            pltpu.VMEM((CHUNKS, 2, n_x - 1, half, chunk), BF16),
            pltpu.VMEM((col_groups, LANES), F32),
            pltpu.VMEM((CHUNKS, groups, LANES), F32),
            pltpu.VMEM((row_groups, LANES), F32),
            pltpu.VMEM((col_groups, LANES), F32),
            pltpu.VMEM((col_groups * 8, LANES), F32),
            pltpu.VMEM((col_groups * 8, LANES), F32),
            pltpu.VMEM((CHUNKS, groups, LANES), F32),
            pltpu.VMEM((ITERS + 1, CHUNKS, groups, LANES), F32),
            pltpu.VMEM((ITERS + 1, CHUNKS, t_peers, groups, LANES), F32),
            pltpu.VMEM((ITERS, col_groups, LANES), F32),
            pltpu.VMEM((ITERS, col_groups, LANES), F32),
            pltpu.VMEM((ITERS, n_z, col_groups, LANES), F32),
            dma((LOADS + 1,)),
            dma((ITERS + 1, CHUNKS)),
            dma((ITERS + 1, CHUNKS)),
            dma((ITERS,)),
            dma((ITERS,)),
            dma((ITERS,)),
            dma((ITERS,)),
            dma((CHUNKS,)),
            dma((CHUNKS,)),
            dma((CHUNKS,)),
            dma((CHUNKS,)),
        ],
        compiler_params=pltpu.CompilerParams(
            collective_id=0, has_side_effects=True, vmem_limit_bytes=213 << 18
        ),
        name="transport",
    )(source_latents, target_latents)
    return moved.T, f.reshape(rows), g.reshape(cols)


def solution(mesh):
    n_src, n_tgt = mesh.shape["src"], mesh.shape["tgt"]
    n_x = math.isqrt(n_tgt)

    def whole(source_latents, target_latents):
        eps = 1.28 / math.sqrt(source_latents.shape[1])
        cfg = (
            n_src // 2,
            n_x,
            n_tgt // n_x,
            eps,
            math.log2(source_latents.shape[0]),
            math.log2(target_latents.shape[0]),
        )
        return jax.shard_map(
            functools.partial(local, cfg),
            mesh=mesh,
            in_specs=(P("src", None), P("tgt", None)),
            out_specs=(P("src", "tgt"), P("src"), P("tgt")),
            check_vma=False,
        )(source_latents, target_latents)

    return whole
```

```python
import functools
import math

import jax
import jax.numpy as jnp
from jax import lax
from jax.experimental import pallas as pl
from jax.experimental.pallas import tpu as pltpu
from jax.sharding import PartitionSpec as P

ITERS = 3
LOADS = 2
CHUNKS = 2
LEAD = 0
LOG2E = math.log2(math.e)
LANES = 128
F32 = jnp.float32
BF16 = jnp.bfloat16
NT_DIMS = (((1,), (1,)), ((), ()))


def ring_distance(k, n):
    return min(k, n - k)


def log2(x):
    return jnp.log(x) * LOG2E


def tree(op, parts):
    while len(parts) > 1:
        paired = [op(p, q) for p, q in zip(parts[::2], parts[1::2])]
        parts = paired + parts[len(parts) - len(parts) % 2 :]
    return parts[0]


def combine(parts):
    top = tree(jnp.maximum, parts)
    return top + log2(tree(jnp.add, [jnp.exp2(p - top) for p in parts]))


def square_sums(block_ref, start, out_ref, row):
    width = block_ref.shape[1]
    total = jnp.zeros((LANES, LANES), F32)
    for c in range(width // LANES):
        piece = block_ref[pl.ds(start, LANES), c * LANES : (c + 1) * LANES].astype(F32)
        total = total + piece * piece
    out_ref[row : row + 1, :] = jnp.sum(total.T, axis=0, keepdims=True)


def kernel(
    cfg,
    src_hbm,
    tgt_hbm,
    moved_ref,
    f_ref,
    g_ref,
    a,
    b,
    b_t,
    scores,
    part,
    column,
    weights,
    sums,
    first_in,
    second_out,
    second_in,
    h_ref,
    u_ref,
    ss_ref,
    tt_ref,
    peak_ref,
    mass_ref,
    own_scale,
    t_send,
    t_recv,
    c_send,
    c_recv,
    z_recv,
    load_sem,
    t_ssem,
    t_rsem,
    c_ssem,
    c_rsem,
    z_ssem,
    z_rsem,
    m_ssem,
    m_rsem,
    n_ssem,
    n_rsem,
):
    n_z, n_x, n_y, eps, log2_rows, log2_cols = cfg
    rows, depth = a.shape
    cols = b.shape[0]
    row_groups, col_groups = rows // LANES, cols // LANES
    s_me, t_me = lax.axis_index("src"), lax.axis_index("tgt")
    z_me, core_me = s_me // 2, s_me % 2
    x_me, y_me = t_me // n_y, t_me % n_y
    half = depth // (n_x * n_y) // 2
    chunk = rows // CHUNKS

    z_steps = sorted(range(1, n_z), key=lambda k: -ring_distance(k, n_z))

    def z_peer(k, core):
        return {"src": ((z_me + k) % n_z) * 2 + core, "tgt": t_me}

    sibling = {"src": z_me * 2 + (1 - core_me), "tgt": t_me}
    steps = [(dx, dy) for dx in range(n_x) for dy in range(n_y) if dx or dy]
    steps.sort(key=lambda d: (-ring_distance(d[0], n_x), -ring_distance(d[1], n_y)))
    t_index = [((x_me + dx) % n_x) * n_y + (y_me + dy) % n_y for dx, dy in steps]
    far = sorted(
        range(len(steps)),
        key=lambda k: -ring_distance(steps[k][0], n_x) - ring_distance(steps[k][1], n_y),
    )

    share = cols // LOADS
    loads = [pltpu.make_async_copy(src_hbm, a, load_sem.at[LOADS])]
    for q in range(LOADS):
        piece = pl.ds(q * share, share)
        loads.append(pltpu.make_async_copy(tgt_hbm.at[piece], b.at[piece], load_sem.at[q]))
    for copy in loads:
        copy.start()

    leads = core_me == LEAD
    barrier = pltpu.get_barrier_semaphore()
    everyone = [z_peer(k, LEAD) for k in z_steps]
    everyone += [{"src": s_me, "tgt": t_index[k]} for k in far] + [sibling]
    for peer in everyone:
        pl.semaphore_signal(
            barrier, inc=1, device_id=peer, device_id_type=pl.DeviceIdType.MESH
        )

    def score(begin, end, q):
        dot = lax.dot_general(
            a[begin:end, :],
            b[q * share : (q + 1) * share, :],
            NT_DIMS,
            preferred_element_type=F32,
        )
        scores[begin:end, q * share : (q + 1) * share] = dot * (
            2.0 * LOG2E / (depth * eps)
        )

    for q in range(LOADS):
        loads[1 + q].wait()
        blocks = range(q * share // LANES, (q + 1) * share // LANES)
        for c in blocks:
            square_sums(b, c * LANES, tt_ref, c)
        if q == 0:
            loads[0].wait()
        if q < LOADS - 1:
            score(0, rows, q)
    h_ref[...] = tt_ref[...] * (-LOG2E / (depth * eps))

    groups = chunk // LANES

    def rows_pass(i, n):
        shift = [
            jnp.broadcast_to(h_ref[c : c + 1, :], (8, LANES)) for c in range(col_groups)
        ]

        for k in range(n * chunk, (n + 1) * chunk, 8):
            v = [
                scores[k : k + 8, c * LANES : (c + 1) * LANES] + shift[c]
                for c in range(col_groups)
            ]
            part[k : k + 8, :] = combine(v)
        for r in range(groups):
            at = n * chunk + r * LANES
            x = part[at : at + LANES, :].T
            top = jnp.max(x, axis=0, keepdims=True)
            t_send[i, n, r : r + 1, :] = top + log2(
                jnp.sum(jnp.exp2(x - top), axis=0, keepdims=True)
            )

    def to_column(ref, n):
        for r in range(groups):
            at = n * chunk + r * LANES
            column[at : at + LANES, :] = jnp.broadcast_to(
                ref[r : r + 1, :], (LANES, LANES)
            ).T

    def start_rows_exchange(i, n):
        for k in far:
            pltpu.make_async_remote_copy(
                src_ref=t_send.at[i, n],
                dst_ref=t_recv.at[i, n, k],
                send_sem=t_ssem.at[i, n],
                recv_sem=t_rsem.at[i, n],
                device_id={"src": s_me, "tgt": t_index[k]},
                device_id_type=pl.DeviceIdType.MESH,
            ).start()

    def wait_bytes(ref, sem):
        pltpu.make_async_copy(ref, ref, sem).wait()

    def columns_pass(i, out_ref):
        shape = (8, LANES)
        low = jnp.full(shape, -3.0e38, F32)
        start = tuple([low] * col_groups + [jnp.zeros(shape, F32)] * col_groups)

        def some_rows(block, carry):
            tops, totals = list(carry[:col_groups]), list(carry[col_groups:])
            at = [pl.ds(pl.multiple_of(block * 64 + k * 8, 8), 8) for k in range(8)]
            u = [column[p, :] for p in at]
            for c in range(col_groups):
                v = [scores[p, c * LANES : (c + 1) * LANES] + w for p, w in zip(at, u)]
                top = jnp.maximum(tree(jnp.maximum, v), tops[c])
                mass = tree(jnp.add, [jnp.exp2(p - top) for p in v])
                totals[c] = totals[c] * jnp.exp2(tops[c] - top) + mass
                tops[c] = top
            return tuple(tops + totals)

        done = start
        for n in range(CHUNKS):
            wait_bytes(t_recv.at[i, n], t_rsem.at[i, n])
            u_ref[n] = -log2_cols - combine(
                [t_send[i, n]] + [t_recv[i, n, k] for k in range(len(steps))]
            )
            to_column(u_ref.at[n], n)
            per = chunk // 64
            done = lax.fori_loop(n * per, (n + 1) * per, some_rows, done, unroll=True)
        for c in range(col_groups):
            peak_ref[c * 8 : (c + 1) * 8, :] = done[c]
            mass_ref[c * 8 : (c + 1) * 8, :] = done[col_groups + c]
        peaks = [peak_ref[pl.ds(r, col_groups, stride=8), :] for r in range(8)]
        masses = [mass_ref[pl.ds(r, col_groups, stride=8), :] for r in range(8)]
        top = tree(jnp.maximum, peaks)
        total = tree(jnp.add, [m * jnp.exp2(p - top) for p, m in zip(peaks, masses)])
        out_ref[...] = top + log2(total)

    for n in range(CHUNKS):
        score(n * chunk, (n + 1) * chunk, LOADS - 1)
    rows_pass(0, 0)

    @pl.when(leads)
    def _():
        pl.semaphore_wait(barrier, len(far) + 1 + 2 * len(z_steps))

    @pl.when(jnp.logical_not(leads))
    def _():
        pl.semaphore_wait(barrier, len(far) + 1)

    start_rows_exchange(0, 0)
    for n in range(1, CHUNKS):
        rows_pass(0, n)
        start_rows_exchange(0, n)

    for r in range(row_groups):
        square_sums(a, r * LANES, ss_ref, r)
    order = sorted(range(n_x), key=lambda d: -ring_distance(d, n_x))

    def position(along):
        return sum(jnp.where(along == e, o, 0) for o, e in enumerate(order))

    def turn(block, carry):
        at = pl.ds(pl.multiple_of(block * LANES, LANES), LANES)
        for c in range(depth // LANES):
            turned = b[at, c * LANES : (c + 1) * LANES].T
            for o in range(LANES // half):
                owner, second = divmod(c * (LANES // half) + o, 2)
                ox, oy = owner // n_y, owner % n_y
                if second:
                    row = position((oy - y_me + n_y) % n_y) * (2 * n_y) + n_y + ox
                else:
                    row = position((ox - x_me + n_x) % n_x) * (2 * n_y) + oy
                b_t[pl.ds(pl.multiple_of(row * half, half), half), at] = turned[
                    o * half : (o + 1) * half
                ]
        return carry

    lax.fori_loop(0, col_groups, turn, 0)

    own_slot = n_z - 1

    def sweep(i, carry):
        columns_pass(i, c_send.at[i])
        copy = pltpu.make_async_remote_copy(
            src_ref=c_send.at[i],
            dst_ref=c_recv.at[i],
            send_sem=c_ssem.at[i],
            recv_sem=c_rsem.at[i],
            device_id=sibling,
            device_id_type=pl.DeviceIdType.MESH,
        )

        @pl.when(jnp.logical_not(leads))
        def _():
            copy.start()
            wait_bytes(z_recv.at[i], z_rsem.at[i])

        @pl.when(leads)
        def _():
            copy.wait_recv()
            z_recv[i, own_slot] = combine([c_send[i], c_recv[i]])

            def send(slot, peer):
                pltpu.make_async_remote_copy(
                    src_ref=z_recv.at[i, own_slot],
                    dst_ref=z_recv.at[i, slot],
                    send_sem=z_ssem.at[i],
                    recv_sem=z_rsem.at[i],
                    device_id=peer,
                    device_id_type=pl.DeviceIdType.MESH,
                ).start()

            for k in z_steps:
                send(k - 1, z_peer(k, 1 - LEAD))
                send(k - 1, z_peer(k, LEAD))
            send(own_slot, sibling)
            wait_bytes(z_recv.at[i, pl.ds(0, own_slot)], z_rsem.at[i])

        h_ref[...] = -log2_rows - combine([z_recv[i, k] for k in range(n_z)])

        @pl.when(i < ITERS - 1)
        def _():
            for n in range(CHUNKS):
                rows_pass(i + 1, n)
                start_rows_exchange(i + 1, n)

        return carry

    lax.fori_loop(0, ITERS, sweep, 0)

    shift = [
        jnp.broadcast_to(h_ref[c : c + 1, :], (16, LANES)) for c in range(col_groups)
    ]

    def weigh(begin, end):
        for k in range(begin, end, 16):
            at = slice(k, k + 16)
            level = column[at, :]
            for c in range(col_groups):
                v = scores[at, c * LANES : (c + 1) * LANES] + shift[c]
                weights[at, c * LANES : (c + 1) * LANES] = jnp.exp2(v - level).astype(BF16)

    band = n_y * half

    def plane_peer(kind, step):
        if kind == 0:
            return {"src": s_me, "tgt": ((x_me + step) % n_x) * n_y + y_me}
        return {"src": s_me, "tgt": x_me * n_y + (y_me + step) % n_y}

    for n in range(CHUNKS):
        rows_pass(ITERS, n)
        start_rows_exchange(ITERS, n)
        to_column(t_send.at[ITERS, n], n)
        weigh(n * chunk, (n + 1) * chunk)
        for o in range(0, n_x, 2):
            at = pl.ds(o * 2 * band, 4 * band)
            dot = lax.dot_general(
                b_t[at, :],
                weights[n * chunk : (n + 1) * chunk, :],
                NT_DIMS,
                preferred_element_type=F32,
            )
            sums[n, at, :] = dot.astype(BF16)
            for p in (o, o + 1):
                for kind in range(2):
                    if order[p]:
                        pltpu.make_async_remote_copy(
                            src_ref=sums.at[n, pl.ds((2 * p + kind) * band, band)],
                            dst_ref=first_in.at[n, kind, order[p] - 1],
                            send_sem=m_ssem.at[n],
                            recv_sem=m_rsem.at[n],
                            device_id=plane_peer(kind, order[p]),
                            device_id_type=pl.DeviceIdType.MESH,
                        ).start()

    for n in range(CHUNKS):
        at = slice(n * groups, (n + 1) * groups)
        f_ref[at, :] = ss_ref[at, :] * (1.0 / depth) + u_ref[n] * (eps / LOG2E)
    g_ref[...] = tt_ref[...] * (1.0 / depth) + h_ref[...] * (eps / LOG2E)

    along = [
        [steps.index((d, 0)) for d in range(1, n_x)],
        [steps.index((0, d)) for d in range(1, n_y)],
    ]
    for n in range(CHUNKS):
        wait_bytes(t_recv.at[ITERS, n], t_rsem.at[ITERS, n])
        level = combine(
            [t_send[ITERS, n]] + [t_recv[ITERS, n, k] for k in range(len(steps))]
        )
        own_scale[n] = jnp.exp2(t_send[ITERS, n] - level)
        for line in along:
            for k in line:
                t_recv[ITERS, n, k] = jnp.exp2(t_recv[ITERS, n, k] - level)

    own = order.index(0)
    lanes = [slice(r * LANES, (r + 1) * LANES) for r in range(chunk // LANES)]
    for n in range(CHUNKS):
        wait_bytes(first_in.at[n], m_rsem.at[n])
        for kind in range(2):
            for r, lane in enumerate(lanes):
                at = pl.ds((2 * own + kind) * band, band)
                total = sums[n, at, lane].astype(F32) * own_scale[n, r : r + 1, :]
                for j, k in enumerate(along[kind]):
                    total += first_in[n, kind, j, :, lane].astype(F32) * t_recv[ITERS, n, k, r : r + 1, :]
                second_out[n, kind, :, lane] = total.astype(BF16)
            for step in order:
                if step:
                    to = (y_me + step) % n_y if kind == 0 else (x_me + step) % n_x
                    pltpu.make_async_remote_copy(
                        src_ref=second_out.at[n, kind, pl.ds(pl.multiple_of(to * half, half), half)],
                        dst_ref=second_in.at[n, kind, step - 1],
                        send_sem=n_ssem.at[n],
                        recv_sem=n_rsem.at[n],
                        device_id=plane_peer(1 - kind, step),
                        device_id_type=pl.DeviceIdType.MESH,
                    ).start()
    for n in range(CHUNKS):
        wait_bytes(second_in.at[n], n_rsem.at[n])
        for kind in range(2):
            me = y_me if kind == 0 else x_me
            mine = pl.ds(pl.multiple_of(me * half, half), half)
            for r, lane in enumerate(lanes):
                total = second_out[n, kind, mine, lane].astype(F32)
                for j in range(n_x - 1):
                    total += second_in[n, kind, j, :, lane].astype(F32)
                at = n * chunk + r * LANES
                moved_ref[kind * half : (kind + 1) * half, at : at + LANES] = total.astype(BF16)

    for i in range(ITERS):

        @pl.when(jnp.logical_not(leads))
        def _():
            wait_bytes(c_send.at[i], c_ssem.at[i])

        @pl.when(leads)
        def _():
            wait_bytes(z_recv.at[i], z_ssem.at[i])
            wait_bytes(z_recv.at[i, pl.ds(0, own_slot)], z_ssem.at[i])

    for i in range(ITERS + 1):
        for n in range(CHUNKS):
            wait_bytes(t_recv.at[i, n], t_ssem.at[i, n])
    for n in range(CHUNKS):
        wait_bytes(first_in.at[n], m_ssem.at[n])
        wait_bytes(second_in.at[n], n_ssem.at[n])


def local(cfg, source_latents, target_latents):
    n_z, n_x, n_y = cfg[:3]
    rows, depth = source_latents.shape
    cols = target_latents.shape[0]
    feats = depth // (n_x * n_y)
    row_groups, col_groups = rows // LANES, cols // LANES
    groups = rows // CHUNKS // LANES
    t_peers = n_x * n_y - 1
    vmem = pl.BlockSpec(memory_space=pltpu.VMEM)
    hbm = pl.BlockSpec(memory_space=pltpu.HBM)
    dma = pltpu.SemaphoreType.DMA
    chunk, half, band = rows // CHUNKS, feats // 2, n_y * feats // 2
    shapes = (
        jax.ShapeDtypeStruct((feats, rows), BF16),
        jax.ShapeDtypeStruct((row_groups, LANES), F32),
        jax.ShapeDtypeStruct((col_groups, LANES), F32),
    )
    moved, f, g = pl.pallas_call(
        functools.partial(kernel, cfg),
        out_shape=shapes,
        in_specs=[hbm, hbm],
        out_specs=(vmem, vmem, vmem),
        scratch_shapes=[
            pltpu.VMEM((rows, depth), BF16),
            pltpu.VMEM((cols, depth), BF16),
            pltpu.VMEM((depth, cols), BF16),
            pltpu.VMEM((rows, cols), F32),
            pltpu.VMEM((rows, LANES), F32),
            pltpu.VMEM((rows, LANES), F32),
            pltpu.VMEM((rows, cols), BF16),
            pltpu.VMEM((CHUNKS, depth, chunk), BF16),
            pltpu.VMEM((CHUNKS, 2, n_x - 1, band, chunk), BF16),
            pltpu.VMEM((CHUNKS, 2, band, chunk), BF16),
            pltpu.VMEM((CHUNKS, 2, n_x - 1, half, chunk), BF16),
            pltpu.VMEM((col_groups, LANES), F32),
            pltpu.VMEM((CHUNKS, groups, LANES), F32),
            pltpu.VMEM((row_groups, LANES), F32),
            pltpu.VMEM((col_groups, LANES), F32),
            pltpu.VMEM((col_groups * 8, LANES), F32),
            pltpu.VMEM((col_groups * 8, LANES), F32),
            pltpu.VMEM((CHUNKS, groups, LANES), F32),
            pltpu.VMEM((ITERS + 1, CHUNKS, groups, LANES), F32),
            pltpu.VMEM((ITERS + 1, CHUNKS, t_peers, groups, LANES), F32),
            pltpu.VMEM((ITERS, col_groups, LANES), F32),
            pltpu.VMEM((ITERS, col_groups, LANES), F32),
            pltpu.VMEM((ITERS, n_z, col_groups, LANES), F32),
            dma((LOADS + 1,)),
            dma((ITERS + 1, CHUNKS)),
            dma((ITERS + 1, CHUNKS)),
            dma((ITERS,)),
            dma((ITERS,)),
            dma((ITERS,)),
            dma((ITERS,)),
            dma((CHUNKS,)),
            dma((CHUNKS,)),
            dma((CHUNKS,)),
            dma((CHUNKS,)),
        ],
        compiler_params=pltpu.CompilerParams(
            collective_id=0, has_side_effects=True, vmem_limit_bytes=213 << 18
        ),
        name="transport",
    )(source_latents, target_latents)
    return moved.T, f.reshape(rows), g.reshape(cols)


def solution(mesh):
    n_src, n_tgt = mesh.shape["src"], mesh.shape["tgt"]
    n_x = math.isqrt(n_tgt)

    def whole(source_latents, target_latents):
        eps = 1.28 / math.sqrt(source_latents.shape[1])
        cfg = (
            n_src // 2,
            n_x,
            n_tgt // n_x,
            eps,
            math.log2(source_latents.shape[0]),
            math.log2(target_latents.shape[0]),
        )
        return jax.shard_map(
            functools.partial(local, cfg),
            mesh=mesh,
            in_specs=(P("src", None), P("tgt", None)),
            out_specs=(P("src", "tgt"), P("src"), P("tgt")),
            check_vma=False,
        )(source_latents, target_latents)

    return whole
```
